32 devices in a mesh: cx: 8 (over y, x, core), tp: 4 (over z).
Axes of the slice: x: 2, y: 2, z: 4, core: 2. Of those that a mesh axis runs over, the one named last changes fastest.
Arguments:
- layer_input: bfloat16 [1024, 3072], P('cx', 'tp'), may hold values from -40 to 40
- queries: bfloat16 [1024, 4096], P('cx', 'tp'), may hold values from -6 to 6
- keys: bfloat16 [1024, 4096], P('cx', 'tp'), may hold values from -6 to 6
- values: bfloat16 [1024, 4096], P('cx', 'tp'), may hold values from -6 to 6
- gate_input: bfloat16 [1024, 4096], P('cx', 'tp'), may hold values from -6 to 6
- log_decay: float32 [32, 1024], P('tp', 'cx'), may hold values from -1 to 0
- prior_state: float32 [32, 128, 128], P('tp'), may hold values from -192 to 192
- attn_gain: float32 [4096], P('tp'), may hold values from 0.5 to 1.5
- out_weight: bfloat16 [4096, 3072], P('tp'), may hold values from -0.09375 to 0.09375
- moe_gain: float32 [3072], replicated, may hold values from 0.5 to 1.5
- router: bfloat16 [3072, 4], replicated, may hold values from -0.109375 to 0.109375
- expert_ids: int32 [1024, 2], P('cx'), may hold values from 0 to 3, all different within a row; in each aligned block of 128 rows (0 to 127, 128 to 255, ...) at most 128 rows name the same one
- w_gate: bfloat16 [8, 3072, 3072], P('cx', None, 'tp'), may hold values from -0.109375 to 0.109375
- w_up: bfloat16 [8, 3072, 3072], P('cx', None, 'tp'), may hold values from -0.109375 to 0.109375
- w_down: bfloat16 [8, 3072, 3072], P('cx', 'tp'), may hold values from -0.078125 to 0.078125
Outputs:
- mixed: bfloat16 [1024, 3072], P('cx', 'tp')
The draws below stay inside these ranges and needn't reach their ends.
Inputs may be any that keep to these rules, and one draw needn't show every extreme that they name: `expert_ids`: each row names 2 different experts. Among the rows of one index of cx no expert is named by more than 128 rows, and in every draw some expert is named by exactly 128 of them.
All inputs are finite; a program needn't handle non-finite values.
Results may differ from the reference program's by a relative error of at most 0.0085.
Values may be sent and summed in bfloat16 or wider, within the bound.
A program may use at most 128 MiB of HBM per device.

```python
import math
import jax
import jax.numpy as jnp
import numpy as np
from jax import lax

D = 3072
HEADS = 32
HEAD = 128
FF = 6144
TOPK = 2
TOK_DEV = 128
EXPERTS = 4
CAP = 128
SPAN_TOKENS = 1024


def draw_log_decay(key, part):
    key = jax.random.fold_in(key, 11)
    flow_lanes = jax.random.split(key, 7)
    fast_share = 0.5
    blocks = SPAN_TOKENS // TOK_DEV
    is_fast = jax.random.uniform(flow_lanes[0], (HEADS, 1)) < fast_share
    fast_rate = jax.random.uniform(flow_lanes[1], (HEADS, 1), minval=1.0 / 50.0, maxval=1.0 / 30.0)
    slow_rate = jax.random.uniform(flow_lanes[2], (HEADS, 1), minval=0.02, maxval=0.07) / SPAN_TOKENS
    rate = jnp.where(is_fast, fast_rate, slow_rate)
    block_factor = jnp.exp(jax.random.uniform(flow_lanes[3], (HEADS, blocks, 1), minval=-0.6931, maxval=0.6931))
    block_factor = jnp.broadcast_to(block_factor, (HEADS, blocks, TOK_DEV)).reshape(HEADS, SPAN_TOKENS)
    jitter = jax.random.uniform(flow_lanes[4], (HEADS, SPAN_TOKENS), minval=0.5, maxval=1.5)
    steady_portion = -rate * block_factor * jitter
    arrival_position = jax.random.randint(flow_lanes[5], (3,), 0, SPAN_TOKENS)
    match_count = (jnp.arange(SPAN_TOKENS)[None, :] == arrival_position[:, None]).astype(jnp.float32)
    kept_entries = jax.random.uniform(flow_lanes[6], (HEADS, 3), minval=0.5, maxval=0.8)
    arrival_groups = jnp.sum(jnp.log(kept_entries)[:, :, None] * match_count[None, :, :], axis=1)
    return steady_portion + arrival_groups


def draw_layer_input(key, part):
    key = jax.random.fold_in(key, 23)
    flow_lanes = jax.random.split(key, 4)
    spread = 0.6
    base = jnp.clip(jax.random.normal(flow_lanes[0], (SPAN_TOKENS, D)), -4.0, 4.0)
    row_scale = jnp.exp(jax.random.uniform(flow_lanes[2], (SPAN_TOKENS, 1), minval=-spread, maxval=spread))
    ramp = jnp.exp(1.0986 * (jnp.arange(D, dtype=jnp.float32)[None, :] / D - 0.5))
    column_scale = ramp * jnp.exp(jax.random.uniform(flow_lanes[3], (1, D), minval=-spread, maxval=spread))
    return (base * row_scale * column_scale).astype(jnp.bfloat16)


def block_scale(stream_key, dims, pieces, low, top_value):
    gain, own = 1.0, jax.random.fold_in(stream_key, 6)
    for dim, parts in pieces:
        heights = jnp.exp(jax.random.uniform(jax.random.fold_in(own, dim), (parts,), jnp.float32, low / len(pieces), top_value / len(pieces)))
        gain = gain * jnp.repeat(heights, dims[dim] // parts).reshape([-1 if axis == dim else 1 for axis in range(len(dims))])
    return gain


def deal_out(stream_key, own, number, rows, count, top, most, skew):
    sequence = jax.random.permutation(stream_key, count)
    packed, usual = shares(count, rows * top, most, skew, True), shares(count, rows * top, most, skew, False)
    places = jnp.arange(count)

    def named(sizes, turn):
        used = int((sizes > 0).sum())
        fixed = max(1, used // 4)
        passed = fixed + (places - fixed + turn * (used - fixed)) % max(1, count - fixed)
        return jnp.zeros((count,), jnp.int32).at[sequence[jnp.where(places < fixed, places, passed)]].set(jnp.asarray(sizes, jnp.int32))

    sizes = jnp.where(number % 4 == 0, named(packed, number // 4), named(usual, number - number // 4 - 1))
    mixed = jax.random.permutation(jax.random.fold_in(own, 3), count)
    giver, receiver = mixed[0:count // 2 * 2:2], mixed[1:count // 2 * 2:2]
    slack = jnp.minimum(sizes[giver] - 1, most - sizes[receiver]) // 2
    slack = jnp.where((giver == sequence[0]) | (receiver == sequence[0]) | (sizes[receiver] == 0), 0, jnp.maximum(slack, 0))
    passed = jax.random.randint(jax.random.fold_in(own, 4), (count // 2,), 0, 1 << 20) % (slack + 1)
    sizes = sizes.at[giver].add(-passed).at[receiver].add(passed)
    items = jnp.searchsorted(jnp.cumsum(sizes), jnp.arange(rows * top), side="right").astype(jnp.int32)
    table = items.reshape(top, rows).T
    table = table[jax.random.permutation(jax.random.fold_in(own, 1), rows)]
    turn = jax.random.randint(jax.random.fold_in(own, 2), (rows, 1), 0, top)
    return jnp.take_along_axis(table, (jnp.arange(top)[None, :] + turn) % top, axis=1)


def shares(number_of, total, limit, slope, full):
    portions = [(1 << 20) // math.isqrt(standing ** slope) + 1 for standing in range(1, number_of + 1)]
    largest = limit if full else min(limit, max(-(-total // number_of), total * portions[0] // sum(portions)))
    least = 1 if total - largest >= number_of - 1 else 0
    holding, spare = [largest] + [least] * (number_of - 1), total - largest - least * (number_of - 1)
    while spare > 0:
        free = [i for i in range(1, number_of) if holding[i] < largest] or [i for i in range(1, number_of) if holding[i] < limit]
        pool, budget = sum([portions[i] for i in free]), spare
        for i in free:
            extra = min(limit - holding[i], max(1, budget * portions[i] // pool), spare)
            holding[i] = holding[i] + extra
            spare = spare - extra
    return np.array(holding)


def gaussian(own_key, extent, deviation, reach, pieces=(), kind=jnp.bfloat16):
    factor_of = block_scale(own_key, extent, pieces, -0.22, 0.18) if pieces else 1.0
    entries = jax.random.normal(own_key, extent, jnp.float32) * deviation * factor_of
    return jnp.minimum(jnp.maximum(entries, -reach), reach).astype(kind)


def setup_inputs(seed: int = 0) -> dict:
    arg_keys = jax.random.split(jax.random.key(seed), 16)
    layer_input = draw_layer_input(jax.random.fold_in(arg_keys[15], 71), 0)
    queries = gaussian(arg_keys[1], (SPAN_TOKENS, HEADS * HEAD), 1.0, 6.0, ((0, 8), (1, 4)))
    keys = gaussian(arg_keys[2], (SPAN_TOKENS, HEADS * HEAD), 1.0, 6.0, ((0, 8), (1, 4)))
    values = gaussian(arg_keys[3], (SPAN_TOKENS, HEADS * HEAD), 1.0, 6.0, ((0, 8), (1, 4)))
    gate_input = gaussian(arg_keys[4], (SPAN_TOKENS, HEADS * HEAD), 1.0, 6.0, ((0, 8), (1, 4)))
    log_decay = draw_log_decay(jax.random.fold_in(arg_keys[15], 71), 0)
    prior_state = gaussian(arg_keys[6], (HEADS, HEAD, HEAD), 32.0, 192.0, ((0, 4),), jnp.float32)
    attn_gain = jnp.clip(1.0 + 0.1 * jax.random.normal(arg_keys[7], (HEADS * HEAD,), jnp.float32), 0.5, 1.5)
    out_weight = gaussian(arg_keys[8], (HEADS * HEAD, D), (HEADS * HEAD) ** -0.5, 0.09375, ((0, 4),))
    moe_gain = jnp.clip(1.0 + 0.1 * jax.random.normal(arg_keys[9], (D,), jnp.float32), 0.5, 1.5)
    router = gaussian(arg_keys[10], (D, EXPERTS), D ** -0.5, 0.109375)
    expert_ids_keys = jax.random.split(jax.random.fold_in(arg_keys[11], 1), SPAN_TOKENS // TOK_DEV)
    expert_ids_turns = jax.random.permutation(jax.random.fold_in(arg_keys[11], 3), SPAN_TOKENS // TOK_DEV)
    expert_ids = jax.vmap(lambda own, number: deal_out(jax.random.fold_in(arg_keys[11], 2), own, number, TOK_DEV, EXPERTS, TOPK, CAP, 2))(expert_ids_keys, expert_ids_turns).reshape((SPAN_TOKENS, TOPK))
    w_gate = gaussian(arg_keys[12], (2 * EXPERTS, D, FF // 2), D ** -0.5, 0.109375, ((0, 8), (2, 4)))
    w_up = gaussian(arg_keys[13], (2 * EXPERTS, D, FF // 2), D ** -0.5, 0.109375, ((0, 8), (2, 4)))
    w_down = gaussian(arg_keys[14], (2 * EXPERTS, FF // 2, D), FF ** -0.5, 0.078125, ((0, 8), (1, 4)))
    return {"layer_input": layer_input, "queries": queries, "keys": keys, "values": values, "gate_input": gate_input, "log_decay": log_decay, "prior_state": prior_state, "attn_gain": attn_gain, "out_weight": out_weight, "moe_gain": moe_gain, "router": router, "expert_ids": expert_ids, "w_gate": w_gate, "w_up": w_up, "w_down": w_down}


epsilon = 1e-06
highest_precision = lax.Precision.HIGHEST

def head_block(carried_state, inputs):
    query_tile, key_tile, value_tile, decay_block = inputs
    running_state = jnp.cumsum(decay_block, axis=1)
    length = running_state.shape[1]
    causal = (jnp.arange(length)[:, None] >= jnp.arange(length)[None, :])[None]
    spread = running_state[:, :, None] - running_state[:, None, :]
    weights = jnp.where(causal, jnp.exp(jnp.where(causal, spread, 0.0)), 0.0)
    scores = jnp.einsum('thk,shk->hts', query_tile, key_tile, precision=highest_precision) * weights
    inner = jnp.einsum('hts,shv->thv', scores, value_tile, precision=highest_precision)
    carried_contribution = jnp.exp(running_state).T[:, :, None] * jnp.einsum('rxg,xgd->rxd', query_tile, carried_state, precision=highest_precision)
    trailing_rows = jnp.exp(running_state[:, -1:] - running_state)
    state_update = jnp.einsum('gpc,gpw->pcw', key_tile * trailing_rows.T[:, :, None], value_tile, precision=highest_precision)
    renewed = jnp.exp(running_state[:, -1])[:, None, None] * carried_state + state_update
    return (renewed, inner + carried_contribution)

def reference(layer_input, queries, keys, values, gate_input, log_decay, prior_state, attn_gain, out_weight, moe_gain, router, expert_ids, w_gate, w_up, w_down):
    blocks = SPAN_TOKENS // TOK_DEV
    query_all = queries.astype(jnp.float32).reshape(blocks, TOK_DEV, HEADS, HEAD)
    key_all = keys.astype(jnp.float32).reshape(blocks, TOK_DEV, HEADS, HEAD)
    value_all = values.astype(jnp.float32).reshape(blocks, TOK_DEV, HEADS, HEAD)
    decay_all = log_decay.reshape(HEADS, blocks, TOK_DEV).transpose(1, 0, 2)
    ending, attended = lax.scan(head_block, prior_state, (query_all, key_all, value_all, decay_all))
    attended = attended.reshape(SPAN_TOKENS, HEADS, HEAD)
    squares = lax.optimization_barrier(jnp.mean(attended * attended, axis=-1, keepdims=True))
    gating = jax.nn.sigmoid(gate_input.astype(jnp.float32).reshape(SPAN_TOKENS, HEADS, HEAD))
    normed = attended * lax.rsqrt(squares + epsilon) * attn_gain.reshape(HEADS, HEAD) * gating
    normed = normed.astype(jnp.bfloat16).reshape(SPAN_TOKENS, HEADS * HEAD)
    hidden_state = layer_input.astype(jnp.float32) + jnp.dot(normed, out_weight, preferred_element_type=jnp.float32)
    row_mean = lax.optimization_barrier(jnp.mean(hidden_state * hidden_state, axis=-1, keepdims=True))
    expert_input = (hidden_state * lax.rsqrt(row_mean + epsilon) * moe_gain).astype(jnp.bfloat16)
    logits = jnp.dot(expert_input, router, preferred_element_type=jnp.float32)
    matched = expert_ids[:, :, None] == jnp.arange(EXPERTS, dtype=jnp.int32)[None, None, :]
    chosen = lax.optimization_barrier(jnp.sum(jnp.where(matched, logits[:, None, :], 0.0), axis=-1))
    margin = chosen[:, 0] - chosen[:, 1]
    mixing = jnp.stack([jax.nn.sigmoid(margin), jax.nn.sigmoid(-margin)], axis=1)
    onehot = matched.reshape(blocks, TOPK * TOK_DEV, EXPERTS).astype(jnp.int32)
    before = jnp.cumsum(onehot, axis=1) - onehot
    position = lax.optimization_barrier(jnp.sum(before * onehot, axis=2)).reshape(blocks, TOK_DEV, TOPK)
    at_slot = position[..., None] == jnp.arange(CAP, dtype=jnp.int32)
    chosen_ids = expert_ids.reshape(blocks, TOK_DEV, TOPK)
    mixing_blocks = mixing.reshape(blocks, TOK_DEV, TOPK)
    expert_float = expert_input.astype(jnp.float32).reshape(blocks, TOK_DEV, D)

    def one_expert(total, inputs):
        index, gate_pair, up_pair, down_pair = inputs
        picked = (chosen_ids == index)[..., None] & at_slot
        dispatch = lax.optimization_barrier(jnp.sum(picked, axis=2)).astype(jnp.float32)
        weighting = lax.optimization_barrier(jnp.sum(jnp.where(picked, mixing_blocks[..., None], 0.0), axis=2))
        routed = jnp.einsum('btc,btd->bcd', dispatch, expert_float, precision=highest_precision)
        routed = routed.astype(jnp.bfloat16).reshape(blocks * CAP, D)
        gate_full = jnp.concatenate([gate_pair[0], gate_pair[1]], axis=1)
        up_full = jnp.concatenate([up_pair[0], up_pair[1]], axis=1)
        down_full = jnp.concatenate([down_pair[0], down_pair[1]], axis=0)
        gated = jnp.dot(routed, gate_full, preferred_element_type=jnp.float32)
        lifted = jnp.dot(routed, up_full, preferred_element_type=jnp.float32)
        activated = (jax.nn.silu(gated) * lifted).astype(jnp.bfloat16)
        produced = jnp.dot(activated, down_full, preferred_element_type=jnp.float32).reshape(blocks, CAP, D)
        return (total + jnp.einsum('btc,bcd->btd', weighting, produced, precision=highest_precision), None)
    start_total = jnp.zeros((blocks, TOK_DEV, D), jnp.float32)
    expert_inputs = (jnp.arange(EXPERTS, dtype=jnp.int32), w_gate.reshape(EXPERTS, 2, D, FF // 2), w_up.reshape(EXPERTS, 2, D, FF // 2), w_down.reshape(EXPERTS, 2, FF // 2, D))
    moe_total, unused = lax.scan(one_expert, start_total, expert_inputs)
    return (hidden_state + moe_total.reshape(SPAN_TOKENS, D)).astype(jnp.bfloat16)
```

```python
import functools

import jax
import jax.numpy as jnp
from jax import lax
from jax.experimental import pallas as pl
from jax.experimental.pallas import tpu as pltpu
from jax.sharding import PartitionSpec as P

epsilon = 1e-06
highest_precision = lax.Precision.HIGHEST


def prefix(shard, axis, combine, identity):
    peers, index = (lax.axis_size(axis), lax.axis_index(axis))
    everything = jax.tree.map(lambda part: lax.all_gather(part, axis), shard)
    start = jax.tree.map(
        lambda part, zero: jnp.broadcast_to(jnp.asarray(zero, part.dtype), part.shape),
        shard,
        identity,
    )

    def lap(k, before):
        reached = k < index
        new = combine(before, jax.tree.map(lambda part: part[k], everything))
        return jax.tree.map(lambda a, b: jnp.where(reached, a, b), new, before)

    return lax.fori_loop(0, peers, lap, start)


def feed_forward(routed, gate_weight, up_weight, down_weight):
    gated = jnp.dot(routed, gate_weight, preferred_element_type=jnp.float32)
    lifted = jnp.dot(routed, up_weight, preferred_element_type=jnp.float32)
    activated = (jax.nn.silu(gated) * lifted).astype(jnp.bfloat16)
    return jnp.dot(activated, down_weight, preferred_element_type=jnp.float32)


def combine_states(earlier, later):
    return (earlier[0] + later[0], jnp.exp(later[0])[:, None, None] * earlier[1] + later[1])


def shards_routed(
    layer_input,
    queries,
    keys,
    values,
    gate_input,
    log_decay,
    prior_state,
    attn_gain,
    out_weight,
    moe_gain,
    router,
    expert_ids,
    w_gate,
    w_up,
    w_down,
):
    positions = queries.shape[0]
    heads_here = log_decay.shape[0]
    head_size = prior_state.shape[1]
    query_vectors = queries.reshape(positions, heads_here, head_size)
    key_rows = keys.reshape(positions, heads_here, head_size)
    value_single_float = values.reshape(positions, heads_here, head_size).astype(jnp.float32)
    running_state = jnp.cumsum(log_decay, axis=1)
    causal = (jnp.arange(positions)[:, None] >= jnp.arange(positions)[None, :])[None]
    spread = running_state[:, :, None] - running_state[:, None, :]
    weights = jnp.where(causal, jnp.exp(jnp.where(causal, spread, 0.0)), 0.0)
    scores = (
        jnp.einsum("thk,shk->hts", query_vectors, key_rows, preferred_element_type=jnp.float32)
        * weights
    )
    inner = jnp.einsum("hts,shv->thv", scores, value_single_float, precision=highest_precision)
    trailing_rows = jnp.exp(running_state[:, -1:] - running_state)
    key_single_float = key_rows.astype(jnp.float32) * trailing_rows.T[:, :, None]
    within_block_state = jnp.einsum(
        "gpc,gpw->pcw", key_single_float, value_single_float, precision=highest_precision
    )
    total_decay = running_state[:, -1]
    identity = (
        jnp.zeros((heads_here,), jnp.float32),
        jnp.zeros((heads_here, head_size, head_size), jnp.float32),
    )
    before_total, before_state = prefix(
        (total_decay, within_block_state), "cx", combine_states, identity
    )
    incoming_state = jnp.exp(before_total)[:, None, None] * prior_state + before_state
    carried_contribution = jnp.exp(running_state).T[:, :, None] * jnp.einsum(
        "rxg,xgd->rxd",
        query_vectors.astype(jnp.float32),
        incoming_state,
        precision=highest_precision,
    )
    attended = inner + carried_contribution
    squares = jnp.mean(attended * attended, axis=-1, keepdims=True)
    gating = jax.nn.sigmoid(
        gate_input.astype(jnp.float32).reshape(positions, heads_here, head_size)
    )
    normed = (
        attended * lax.rsqrt(squares + epsilon) * attn_gain.reshape(heads_here, head_size) * gating
    )
    normed = normed.astype(jnp.bfloat16).reshape(positions, heads_here * head_size)
    partial_rows = jnp.dot(normed, out_weight, preferred_element_type=jnp.float32)
    model_width = out_weight.shape[1]
    width_share = layer_input.shape[1]
    column_start = lax.axis_index("tp") * width_share
    own_columns = lax.dynamic_slice_in_dim(
        partial_rows, column_start, width_share, 1
    ) + layer_input.astype(jnp.float32)
    partial_rows = lax.dynamic_update_slice_in_dim(partial_rows, own_columns, column_start, 1)
    expert_count = router.shape[1]
    hidden_state = lax.psum(partial_rows, "tp")
    row_mean = jnp.mean(hidden_state * hidden_state, axis=-1, keepdims=True)
    full_input = (hidden_state * lax.rsqrt(row_mean + epsilon) * moe_gain).astype(jnp.bfloat16)
    logits = jnp.dot(full_input, router, preferred_element_type=jnp.float32)
    hidden_share = lax.dynamic_slice_in_dim(hidden_state, column_start, width_share, 1)
    matched = expert_ids[:, :, None] == jnp.arange(expert_count, dtype=jnp.int32)[None, None, :]
    chosen = jnp.sum(jnp.where(matched, logits[:, None, :], 0.0), axis=-1)
    margin = chosen[:, 0] - chosen[:, 1]
    mixing = jnp.stack([jax.nn.sigmoid(margin), jax.nn.sigmoid(-margin)], axis=1)
    choices_made = expert_ids.shape[1]
    onehot = matched.reshape(positions * choices_made, expert_count).astype(jnp.int32)
    before = jnp.cumsum(onehot, axis=0) - onehot
    position = jnp.sum(before * onehot, axis=1).reshape(positions, choices_made)
    capacity = 8 * positions // lax.axis_size("cx")
    at_slot = position[:, :, None] == jnp.arange(capacity, dtype=jnp.int32)[None, None, :]
    picked = matched[:, :, :, None] & at_slot[:, :, None, :]
    dispatch = (
        jnp.sum(picked, axis=1).astype(jnp.bfloat16).reshape(positions, expert_count * capacity)
    )
    weighting = jnp.sum(jnp.where(picked, mixing[:, :, None, None], 0.0), axis=1).reshape(
        positions, expert_count * capacity
    )
    gate_weight = w_gate[0]
    up_weight = w_up[0]
    down_weight = w_down[0]
    outgoing = jnp.einsum(
        "tm,td->md", dispatch, full_input, preferred_element_type=jnp.float32
    ).astype(jnp.bfloat16)
    outgoing = jnp.repeat(outgoing.reshape(expert_count, capacity, model_width), 2, axis=0)
    received = lax.all_to_all(outgoing, "cx", split_axis=0, concat_axis=0, tiled=True)
    owners, slots, columns = received.shape
    produced = feed_forward(
        received.reshape(owners * slots, columns), gate_weight, up_weight, down_weight
    )
    returned = lax.all_to_all(
        produced.reshape(owners, slots, columns).astype(jnp.bfloat16),
        "cx",
        split_axis=0,
        concat_axis=0,
        tiled=True,
    ).astype(jnp.float32)
    halves = jnp.sum(returned.reshape(expert_count, 2, capacity, model_width), axis=1)
    moe_rows = jnp.dot(
        weighting,
        halves.reshape(expert_count * capacity, model_width),
        precision=highest_precision,
        preferred_element_type=jnp.float32,
    )
    moe_share = lax.psum_scatter(
        moe_rows.astype(jnp.bfloat16), "tp", scatter_dimension=1, tiled=True
    ).astype(jnp.float32)
    return (hidden_share + moe_share).astype(jnp.bfloat16)


MESH = pl.DeviceIdType.MESH
VMEM_BYTES = 46 * 1024 * 1024
CHIPS = 4
PIECES = 4


def neighbours():
    cx, tp = lax.axis_index("cx"), lax.axis_index("tp")
    sibling = cx + 1 - 2 * (cx % 2)
    along_x = cx + 2 - 4 * ((cx // 2) % 2)
    along_y = (cx + 4) % 8
    return cx, tp, sibling, along_x, along_y


def partners(tp):
    return [tp, tp + 1 - 2 * (tp % 2), (tp + 2) % 4, 3 - tp]


def greet(devices):
    barrier = pltpu.get_barrier_semaphore()
    for device in devices:
        pl.semaphore_signal(barrier, inc=1, device_id=device, device_id_type=MESH)
    pl.semaphore_wait(barrier, len(devices))


class Copies:
    def __init__(self, send, recv):
        self.send, self.recv, self.numbers, self.started = send, recv, {}, []

    def make(self, name, source, target, device):
        number = self.numbers.setdefault(name, len(self.numbers))
        return pltpu.make_async_remote_copy(
            src_ref=source,
            dst_ref=target,
            send_sem=self.send.at[number],
            recv_sem=self.recv.at[number],
            device_id=device,
            device_id_type=MESH,
        )

    def start(self, name, source, target, device):
        copy = self.make(name, source, target, device)
        copy.start()
        self.started.append(copy)

    def wait(self, name, landed, device):
        self.make(name, landed, landed, device).wait_recv()

    def drain(self):
        for copy in self.started:
            copy.wait_send()


def plane_gather(copies, place, rows, split):
    cx, tp, sibling, along_x, along_y = neighbours()
    across = (along_x + 4) % 8
    to_sibling, to_x, to_y = (sibling, tp), (along_x, tp), (along_y, tp)
    parts = ((0, split), (split, rows - split))

    def pair(owner):
        return owner + 1 - 2 * (owner % 2)

    def push(name, owner, piece, part, device):
        ref = place(owner, piece, *part)
        copies.start(name, ref, ref, device)

    def arrive(name, owner, piece, part):
        copies.wait(name, place(owner, piece, *part), to_sibling)

    whole = (0, rows)

    def stage(j, piece):
        push(("x", j), cx, piece, whole, to_x)
        push(("y", j), cx, piece, whole, to_y)
        push(("own", j), cx, piece, whole, to_sibling)

    def forward(j, piece):
        arrive(("x", j), along_x, piece, whole)
        push(("dy", j), along_x, piece, parts[0], to_y)
        push(("sx", j), along_x, piece, whole, to_sibling)
        arrive(("y", j), along_y, piece, whole)
        push(("dx", j), along_y, piece, parts[1], to_x)
        push(("sy", j), along_y, piece, whole, to_sibling)

    def corner(j, piece):
        arrive(("dy", j), across, piece, parts[0])
        push(("sd0", j), across, piece, parts[0], to_sibling)
        arrive(("dx", j), across, piece, parts[1])
        push(("sd1", j), across, piece, parts[1], to_sibling)

    def finish(j, piece, which):
        if which == 0:
            arrive(("own", j), pair(cx), piece, whole)
        if which == 1:
            arrive(("sx", j), pair(along_x), piece, whole)
            arrive(("sy", j), pair(along_y), piece, whole)
        if which == 2:
            arrive(("sd0", j), pair(across), piece, parts[0])
            arrive(("sd1", j), pair(across), piece, parts[1])

    return stage, forward, corner, finish


def state_kernel(rows, split, block_ref, all_ref, last_ref, send, recv, local):
    cx, tp, sibling, along_x, along_y = neighbours()
    own = pltpu.make_async_copy(block_ref, all_ref.at[cx], local)
    own.start()
    greet([(sibling, tp), (along_x, tp), (along_y, tp)])
    own.wait()
    copies = Copies(send, recv)

    def place(owner, piece, first, count):
        return all_ref.at[owner, pl.ds(first, count), :]

    stage, forward, corner, finish = plane_gather(copies, place, rows, split)
    stage(0, 0)
    forward(0, 0)
    corner(0, 0)
    for which in range(3):
        finish(0, 0, which)
    last_ref[...] = all_ref[:, rows - 16 :, :].astype(jnp.float32)
    copies.drain()


def gather_states(block):
    rows = block.shape[0]
    return pl.pallas_call(
        functools.partial(state_kernel, rows, rows // 32 * 16),
        out_shape=(
            jax.ShapeDtypeStruct((2 * CHIPS,) + block.shape, block.dtype),
            jax.ShapeDtypeStruct((2 * CHIPS, 16, block.shape[1]), jnp.float32),
        ),
        in_specs=[pl.BlockSpec(memory_space=pltpu.VMEM)],
        out_specs=(pl.BlockSpec(memory_space=pltpu.VMEM), pl.BlockSpec(memory_space=pltpu.VMEM)),
        scratch_shapes=[
            pltpu.SemaphoreType.DMA((9,)),
            pltpu.SemaphoreType.DMA((9,)),
            pltpu.SemaphoreType.DMA,
        ],
        compiler_params=pltpu.CompilerParams(
            collective_id=1, has_side_effects=True, vmem_limit_bytes=VMEM_BYTES
        ),
        name="gather_states",
    )(block)


def layer_kernel(
    partial_ref,
    layer_ref,
    gain_ref,
    router_ref,
    ids_ref,
    gate_hbm,
    up_hbm,
    down_hbm,
    out_ref,
    hidden_ref,
    all_ref,
    squares,
    gate_ref,
    up_ref,
    down_ref,
    activated,
    produced_ref,
    paired,
    outbox,
    inbox,
    corner_out,
    x_out,
    y_out,
    corner_x,
    corner_y,
    x_in,
    y_in,
    z_out,
    z_in,
    send,
    recv,
    local,
):
    cx, tp, sibling, along_x, along_y = neighbours()
    rows, share = layer_ref.shape
    hidden_units = down_ref.shape[0]
    width = down_ref.shape[1]
    half = rows // 2
    top, low = pl.ds(0, half), pl.ds(half, half)
    peers = partners(tp)
    across = (along_x + 4) % 8
    to_sibling, to_x, to_y = (sibling, tp), (along_x, tp), (along_y, tp)
    loads = [
        pltpu.make_async_copy(source, target, local.at[k])
        for k, (source, target) in enumerate(
            ((gate_hbm, gate_ref), (up_hbm, up_ref), (down_hbm, down_ref))
        )
    ]
    for load in loads:
        load.start()
    greet([to_sibling, to_x, to_y] + [(cx, peer) for peer in peers[1:]])
    copies = Copies(send, recv)

    def columns(piece):
        return pl.ds(pl.multiple_of(piece * share, share), share)

    outbox[3] = partial_ref[:, columns(peers[3])].astype(jnp.bfloat16)
    copies.start(("sum", 3), outbox.at[3], inbox.at[2], (cx, peers[1]))
    outbox[1] = partial_ref[:, columns(peers[1])].astype(jnp.bfloat16)
    copies.start(("sum", 1), outbox.at[1], inbox.at[1], (cx, peers[1]))
    hidden = partial_ref[:, columns(tp)] + layer_ref[...].astype(jnp.float32)
    copies.wait(("sum", 3), inbox.at[2], (cx, peers[1]))
    outbox[2] = (partial_ref[:, columns(peers[2])] + inbox[2].astype(jnp.float32)).astype(
        jnp.bfloat16
    )
    copies.start(("sum", 2), outbox.at[2], inbox.at[3], (cx, peers[2]))
    copies.wait(("sum", 1), inbox.at[1], (cx, peers[1]))
    hidden = hidden + inbox[1].astype(jnp.float32)
    copies.wait(("sum", 2), inbox.at[3], (cx, peers[2]))
    hidden = hidden + inbox[3].astype(jnp.float32)
    hidden_ref[...] = hidden
    squares[0] = lax.dot_general(
        jnp.ones((8, share), jnp.float32),
        hidden * hidden,
        (((1,), (1,)), ((), ())),
        precision=highest_precision,
        preferred_element_type=jnp.float32,
    )
    for j in (3, 2, 1):
        copies.start(("squares", j), squares.at[0], squares.at[j], (cx, peers[j]))
    total = squares[0]
    for j in (1, 2, 3):
        copies.wait(("squares", j), squares.at[j], (cx, peers[j]))
        total = total + squares[j]
    scale = lax.rsqrt(total / (share * PIECES) + epsilon)
    scale = jnp.transpose(jnp.broadcast_to(scale[0:1, :], (rows, rows)))[:, 0:1]
    first_row = pl.multiple_of(cx * rows, rows)
    all_ref[pl.ds(first_row, rows), columns(tp)] = (
        hidden_ref[...] * scale * gain_ref[:, columns(tp)]
    ).astype(jnp.bfloat16)

    def place(owner, piece, start, count):
        return all_ref.at[
            pl.ds(pl.multiple_of(owner * rows + start, 16), count), columns(piece)
        ]

    stage, forward, corner, finish = plane_gather(copies, place, rows, half)
    mine = place(cx, tp, 0, rows)
    for j in (2, 1):
        copies.start(("z", j), mine, mine, (cx, peers[j]))
    stage(0, peers[0])

    def take(j):
        landed = place(cx, peers[j], 0, rows)
        copies.wait(("z", j), landed, (cx, peers[j]))
        if j == 2:
            copies.start(("z", 3), landed, landed, (cx, peers[1]))
        stage(j, peers[j])

    expert = (cx // 2).astype(jnp.float32)
    expert_count = router_ref.shape[1]

    def choice(owner):
        first, second = [
            jnp.transpose(jnp.broadcast_to(ids_ref[owner, k : k + 1, :], (rows, rows)))[
                :, :expert_count
            ]
            for k in range(2)
        ]
        lanes = lax.broadcasted_iota(jnp.int32, (rows, expert_count), 1).astype(jnp.float32)

        def equal(a, b):
            return jnp.where(a == b, 1.0, 0.0)

        return (equal(first, lanes) - equal(second, lanes)) * (
            equal(first, expert) - equal(second, expert)
        )

    def compute(owner):
        start = pl.multiple_of(owner // 2 * (2 * rows), 2 * rows)
        here = pl.ds(start, 2 * rows)
        logits = jnp.dot(all_ref[here], router_ref[...], preferred_element_type=jnp.float32)
        select = jnp.concatenate([choice(start // rows), choice(start // rows + 1)])
        weight = jax.nn.sigmoid(jnp.sum(logits * select, axis=1, keepdims=True))
        weight = weight * (0.5 * jnp.sum(select * select, axis=1, keepdims=True))

        def lift(n, carry):
            units = pl.ds(pl.multiple_of(n * 256, 256), 256)
            gated = jnp.dot(
                all_ref[here], gate_ref[:, units], preferred_element_type=jnp.float32
            )
            lifted = jnp.dot(all_ref[here], up_ref[:, units], preferred_element_type=jnp.float32)
            activated[:, units] = (gated * jax.nn.sigmoid(gated) * lifted).astype(jnp.bfloat16)
            return carry

        lax.fori_loop(0, hidden_units // 256, lift, 0)

        def lower(n, carry):
            span = pl.ds(pl.multiple_of(n * 512, 512), 512)
            product = jnp.dot(
                activated[...], down_ref[:, span], preferred_element_type=jnp.float32
            )
            produced_ref[here, span] = (product * weight).astype(jnp.bfloat16)
            return carry

        lax.fori_loop(0, width // 512, lower, 0)

    homes = (across, along_x, along_y, cx)
    order = (3, 2, 1, 0)

    def part(owner, j):
        return produced_ref.at[
            pl.ds(pl.multiple_of(owner * rows, rows), rows), columns(peers[j])
        ]

    def trade(k):
        other = homes[k] + 1 - 2 * (homes[k] % 2)
        for j in order:
            copies.start(("pair", j, k), part(other, j), paired.at[j, k], to_sibling)

    def both(j, k):
        copies.wait(("pair", j, k), paired.at[j, k], to_sibling)
        return part(homes[k], j)[...].astype(jnp.float32) + paired[j, k].astype(jnp.float32)

    def send_x(j):
        x_out[j] = both(j, 1).astype(jnp.bfloat16)
        copies.start(("x0", j), x_out.at[j, top], x_in.at[j, top], to_x)

    def send_y(j):
        y_out[j] = both(j, 2).astype(jnp.bfloat16)
        copies.start(("y1", j), y_out.at[j, low], y_in.at[j, low], to_y)

    def send_corner(j):
        corner_out[j] = both(j, 0).astype(jnp.bfloat16)
        copies.start(("cx", j), corner_out.at[j, top], corner_x.at[j], to_x)
        copies.start(("cy", j), corner_out.at[j, low], corner_y.at[j], to_y)

    def second(j):
        copies.wait(("cx", j), corner_x.at[j], to_x)
        y_out[j, top] = (
            y_out[j, top].astype(jnp.float32) + corner_x[j].astype(jnp.float32)
        ).astype(jnp.bfloat16)
        copies.start(("y0", j), y_out.at[j, top], y_in.at[j, top], to_y)
        copies.wait(("cy", j), corner_y.at[j], to_y)
        x_out[j, low] = (
            x_out[j, low].astype(jnp.float32) + corner_y[j].astype(jnp.float32)
        ).astype(jnp.bfloat16)
        copies.start(("x1", j), x_out.at[j, low], x_in.at[j, low], to_x)

    def third(j):
        total = both(j, 3)
        copies.wait(("x0", j), x_in.at[j, top], to_x)
        copies.wait(("y1", j), y_in.at[j, low], to_y)
        copies.wait(("y0", j), y_in.at[j, top], to_y)
        copies.wait(("x1", j), x_in.at[j, low], to_x)
        total = total + x_in[j].astype(jnp.float32) + y_in[j].astype(jnp.float32)
        if j == 2:
            copies.wait(("z_out", 3), z_in.at[2], (cx, peers[1]))
            total = total + z_in[2].astype(jnp.float32)
        if j:
            slot, peer = {3: (2, 1), 2: (3, 2), 1: (1, 1)}[j]
            z_out[j] = total.astype(jnp.bfloat16)
            copies.start(("z_out", j), z_out.at[j], z_in.at[slot], (cx, peers[peer]))
        return total

    take(1)
    forward(0, peers[0])
    take(2)
    forward(1, peers[1])
    corner(0, peers[0])
    take(3)
    forward(2, peers[2])
    corner(1, peers[1])
    for load in loads:
        load.wait()
    for j in range(PIECES):
        finish(j, peers[j], 0)
    compute(cx)
    trade(3)
    forward(3, peers[3])
    corner(2, peers[2])
    for j in range(PIECES):
        finish(j, peers[j], 1)
    compute(along_x)
    trade(1)
    corner(3, peers[3])
    compute(along_y)
    trade(2)
    for j in order:
        send_x(j)
    for j in range(PIECES):
        finish(j, peers[j], 2)
    compute(across)
    trade(0)
    for j in order:
        send_y(j)
    for j in order:
        send_corner(j)
    second(3)
    second(2)
    third(3)
    second(1)
    second(0)
    third(2)
    third(1)
    total = third(0) + hidden_ref[...]
    copies.wait(("z_out", 1), z_in.at[1], (cx, peers[1]))
    copies.wait(("z_out", 2), z_in.at[3], (cx, peers[2]))
    total = total + z_in[1].astype(jnp.float32) + z_in[3].astype(jnp.float32)
    out_ref[...] = total.astype(jnp.bfloat16)
    copies.drain()


def experts_layer(partial_rows, layer_input, gain, router, ids, w_gate, w_up, w_down):
    rows, share = layer_input.shape
    width, units = w_gate.shape
    everyone = 2 * CHIPS * rows
    in_vmem = pl.BlockSpec(memory_space=pltpu.VMEM)
    anywhere = pl.BlockSpec(memory_space=pl.ANY)
    piece = pltpu.VMEM((PIECES, rows, share), jnp.bfloat16)
    half = pltpu.VMEM((PIECES, rows // 2, share), jnp.bfloat16)
    work = everyone * 6 * width * units
    return pl.pallas_call(
        layer_kernel,
        out_shape=jax.ShapeDtypeStruct((rows, share), jnp.bfloat16),
        in_specs=[in_vmem] * 5 + [anywhere] * 3,
        out_specs=in_vmem,
        scratch_shapes=[
            pltpu.VMEM((rows, share), jnp.float32),
            pltpu.VMEM((everyone, width), jnp.bfloat16),
            pltpu.VMEM((PIECES, 8, rows), jnp.float32),
            pltpu.VMEM((width, units), jnp.bfloat16),
            pltpu.VMEM((width, units), jnp.bfloat16),
            pltpu.VMEM((units, width), jnp.bfloat16),
            pltpu.VMEM((2 * rows, units), jnp.bfloat16),
            pltpu.VMEM((everyone, width), jnp.bfloat16),
            pltpu.VMEM((PIECES, CHIPS, rows, share), jnp.bfloat16),
        ]
        + [piece] * 5
        + [half] * 2
        + [piece] * 4
        + [pltpu.SemaphoreType.DMA((88,)), pltpu.SemaphoreType.DMA((88,))]
        + [pltpu.SemaphoreType.DMA((3,))],
        compiler_params=pltpu.CompilerParams(
            collective_id=2, has_side_effects=True, vmem_limit_bytes=VMEM_BYTES
        ),
        cost_estimate=pl.CostEstimate(
            flops=work, bytes_accessed=6 * width * units, transcendentals=0
        ),
        name="experts_layer",
    )(partial_rows, layer_input, gain, router, ids, w_gate, w_up, w_down)


def shards_dense(
    layer_input,
    queries,
    keys,
    values,
    gate_input,
    log_decay,
    prior_state,
    attn_gain,
    out_weight,
    moe_gain,
    router,
    expert_ids,
    w_gate,
    w_up,
    w_down,
):
    positions = queries.shape[0]
    heads_here = log_decay.shape[0]
    head_size = prior_state.shape[1]
    me = lax.axis_index("cx")
    query_vectors = queries.reshape(positions, heads_here, head_size)
    key_rows = keys.reshape(positions, heads_here, head_size)
    value_single_float = values.reshape(positions, heads_here, head_size).astype(jnp.float32)
    running_state = jnp.cumsum(log_decay, axis=1)
    trailing_rows = jnp.exp(running_state[:, -1:] - running_state)
    key_single_float = key_rows.astype(jnp.float32) * trailing_rows.T[:, :, None]
    within_block_state = jnp.einsum(
        "gpc,gpw->pcw", key_single_float, value_single_float, precision=highest_precision
    )
    total_decay = running_state[:, -1]
    coarse = lax.reduce_precision(total_decay, 8, 7)
    decay_row = jnp.concatenate(
        [coarse, total_decay - coarse, jnp.zeros((head_size - 2 * heads_here,), jnp.float32)]
    )
    extra = jnp.concatenate(
        [
            expert_ids.T.astype(jnp.float32),
            decay_row[None, :],
            jnp.zeros((13, head_size), jnp.float32),
        ]
    )
    state_rows = heads_here * head_size
    block = jnp.concatenate(
        [within_block_state.reshape(state_rows, head_size), extra]
    ).astype(jnp.bfloat16)
    gathered, all_ids = gather_states(block)
    decays = all_ids[:, 2, :]
    decays = decays[:, :heads_here] + decays[:, heads_here : 2 * heads_here]
    peers = decays.shape[0]
    spot = jnp.arange(peers)
    earlier = spot < me
    decays = jnp.where(earlier[:, None], decays, 0.0)
    later = spot[None, :] > spot[:, None]
    factor = jnp.exp(jnp.sum(jnp.where(later[:, :, None], decays[None], 0.0), axis=1))
    factor = jnp.where(earlier[:, None], factor, 0.0)
    all_states = gathered[:, :state_rows, :].reshape(peers, heads_here, head_size, head_size)
    incoming_state = jnp.exp(jnp.sum(decays, axis=0))[:, None, None] * prior_state + jnp.sum(
        factor[:, :, None, None] * all_states.astype(jnp.float32), axis=0
    )
    causal = (jnp.arange(positions)[:, None] >= jnp.arange(positions)[None, :])[None]
    spread = running_state[:, :, None] - running_state[:, None, :]
    weights = jnp.where(causal, jnp.exp(jnp.where(causal, spread, 0.0)), 0.0)
    scores = (
        jnp.einsum("thk,shk->hts", query_vectors, key_rows, preferred_element_type=jnp.float32)
        * weights
    )
    inner = jnp.einsum("hts,shv->thv", scores, value_single_float, precision=highest_precision)
    carried_contribution = jnp.exp(running_state).T[:, :, None] * jnp.einsum(
        "rxg,xgd->rxd",
        query_vectors.astype(jnp.float32),
        incoming_state,
        precision=highest_precision,
    )
    attended = inner + carried_contribution
    squares = jnp.mean(attended * attended, axis=-1, keepdims=True)
    gating = jax.nn.sigmoid(
        gate_input.astype(jnp.float32).reshape(positions, heads_here, head_size)
    )
    normed = (
        attended * lax.rsqrt(squares + epsilon) * attn_gain.reshape(heads_here, head_size) * gating
    )
    normed = normed.astype(jnp.bfloat16).reshape(positions, heads_here * head_size)
    partial_rows = jnp.dot(normed, out_weight, preferred_element_type=jnp.float32)
    return experts_layer(
        partial_rows, layer_input, moe_gain[None, :], router, all_ids, w_gate[0], w_up[0], w_down[0]
    )


def solution(mesh):
    placed = (
        P("cx", "tp"),
        P("cx", "tp"),
        P("cx", "tp"),
        P("cx", "tp"),
        P("cx", "tp"),
        P("tp", "cx"),
        P("tp", None, None),
        P("tp"),
        P("tp", None),
        P(),
        P(),
        P("cx", None),
        P("cx", None, "tp"),
        P("cx", None, "tp"),
        P("cx", "tp", None),
    )
    dense = mesh.shape["cx"] == 2 * CHIPS and mesh.shape["tp"] == PIECES
    shards = shards_dense if dense else shards_routed
    return jax.shard_map(
        shards, mesh=mesh, in_specs=placed, out_specs=P("cx", "tp"), check_vma=False
    )
```

```python
import functools

import jax
import jax.numpy as jnp
from jax import lax
from jax.experimental import pallas as pl
from jax.experimental.pallas import tpu as pltpu
from jax.sharding import PartitionSpec as P

epsilon = 1e-06
highest_precision = lax.Precision.HIGHEST


def prefix(shard, axis, combine, identity):
    peers, index = (lax.axis_size(axis), lax.axis_index(axis))
    everything = jax.tree.map(lambda part: lax.all_gather(part, axis), shard)
    start = jax.tree.map(
        lambda part, zero: jnp.broadcast_to(jnp.asarray(zero, part.dtype), part.shape),
        shard,
        identity,
    )

    def lap(k, before):
        reached = k < index
        new = combine(before, jax.tree.map(lambda part: part[k], everything))
        return jax.tree.map(lambda a, b: jnp.where(reached, a, b), new, before)

    return lax.fori_loop(0, peers, lap, start)


def feed_forward(routed, gate_weight, up_weight, down_weight):
    gated = jnp.dot(routed, gate_weight, preferred_element_type=jnp.float32)
    lifted = jnp.dot(routed, up_weight, preferred_element_type=jnp.float32)
    activated = (jax.nn.silu(gated) * lifted).astype(jnp.bfloat16)
    return jnp.dot(activated, down_weight, preferred_element_type=jnp.float32)


def combine_states(earlier, later):
    return (earlier[0] + later[0], jnp.exp(later[0])[:, None, None] * earlier[1] + later[1])


def shards_routed(
    layer_input,
    queries,
    keys,
    values,
    gate_input,
    log_decay,
    prior_state,
    attn_gain,
    out_weight,
    moe_gain,
    router,
    expert_ids,
    w_gate,
    w_up,
    w_down,
):
    positions = queries.shape[0]
    heads_here = log_decay.shape[0]
    head_size = prior_state.shape[1]
    query_vectors = queries.reshape(positions, heads_here, head_size)
    key_rows = keys.reshape(positions, heads_here, head_size)
    value_single_float = values.reshape(positions, heads_here, head_size).astype(jnp.float32)
    running_state = jnp.cumsum(log_decay, axis=1)
    causal = (jnp.arange(positions)[:, None] >= jnp.arange(positions)[None, :])[None]
    spread = running_state[:, :, None] - running_state[:, None, :]
    weights = jnp.where(causal, jnp.exp(jnp.where(causal, spread, 0.0)), 0.0)
    scores = (
        jnp.einsum("thk,shk->hts", query_vectors, key_rows, preferred_element_type=jnp.float32)
        * weights
    )
    inner = jnp.einsum("hts,shv->thv", scores, value_single_float, precision=highest_precision)
    trailing_rows = jnp.exp(running_state[:, -1:] - running_state)
    key_single_float = key_rows.astype(jnp.float32) * trailing_rows.T[:, :, None]
    within_block_state = jnp.einsum(
        "gpc,gpw->pcw", key_single_float, value_single_float, precision=highest_precision
    )
    total_decay = running_state[:, -1]
    identity = (
        jnp.zeros((heads_here,), jnp.float32),
        jnp.zeros((heads_here, head_size, head_size), jnp.float32),
    )
    before_total, before_state = prefix(
        (total_decay, within_block_state), "cx", combine_states, identity
    )
    incoming_state = jnp.exp(before_total)[:, None, None] * prior_state + before_state
    carried_contribution = jnp.exp(running_state).T[:, :, None] * jnp.einsum(
        "rxg,xgd->rxd",
        query_vectors.astype(jnp.float32),
        incoming_state,
        precision=highest_precision,
    )
    attended = inner + carried_contribution
    squares = jnp.mean(attended * attended, axis=-1, keepdims=True)
    gating = jax.nn.sigmoid(
        gate_input.astype(jnp.float32).reshape(positions, heads_here, head_size)
    )
    normed = (
        attended * lax.rsqrt(squares + epsilon) * attn_gain.reshape(heads_here, head_size) * gating
    )
    normed = normed.astype(jnp.bfloat16).reshape(positions, heads_here * head_size)
    partial_rows = jnp.dot(normed, out_weight, preferred_element_type=jnp.float32)
    model_width = out_weight.shape[1]
    width_share = layer_input.shape[1]
    column_start = lax.axis_index("tp") * width_share
    own_columns = lax.dynamic_slice_in_dim(
        partial_rows, column_start, width_share, 1
    ) + layer_input.astype(jnp.float32)
    partial_rows = lax.dynamic_update_slice_in_dim(partial_rows, own_columns, column_start, 1)
    expert_count = router.shape[1]
    hidden_state = lax.psum(partial_rows, "tp")
    row_mean = jnp.mean(hidden_state * hidden_state, axis=-1, keepdims=True)
    full_input = (hidden_state * lax.rsqrt(row_mean + epsilon) * moe_gain).astype(jnp.bfloat16)
    logits = jnp.dot(full_input, router, preferred_element_type=jnp.float32)
    hidden_share = lax.dynamic_slice_in_dim(hidden_state, column_start, width_share, 1)
    matched = expert_ids[:, :, None] == jnp.arange(expert_count, dtype=jnp.int32)[None, None, :]
    chosen = jnp.sum(jnp.where(matched, logits[:, None, :], 0.0), axis=-1)
    margin = chosen[:, 0] - chosen[:, 1]
    mixing = jnp.stack([jax.nn.sigmoid(margin), jax.nn.sigmoid(-margin)], axis=1)
    choices_made = expert_ids.shape[1]
    onehot = matched.reshape(positions * choices_made, expert_count).astype(jnp.int32)
    before = jnp.cumsum(onehot, axis=0) - onehot
    position = jnp.sum(before * onehot, axis=1).reshape(positions, choices_made)
    capacity = 8 * positions // lax.axis_size("cx")
    at_slot = position[:, :, None] == jnp.arange(capacity, dtype=jnp.int32)[None, None, :]
    picked = matched[:, :, :, None] & at_slot[:, :, None, :]
    dispatch = (
        jnp.sum(picked, axis=1).astype(jnp.bfloat16).reshape(positions, expert_count * capacity)
    )
    weighting = jnp.sum(jnp.where(picked, mixing[:, :, None, None], 0.0), axis=1).reshape(
        positions, expert_count * capacity
    )
    gate_weight = w_gate[0]
    up_weight = w_up[0]
    down_weight = w_down[0]
    outgoing = jnp.einsum(
        "tm,td->md", dispatch, full_input, preferred_element_type=jnp.float32
    ).astype(jnp.bfloat16)
    outgoing = jnp.repeat(outgoing.reshape(expert_count, capacity, model_width), 2, axis=0)
    received = lax.all_to_all(outgoing, "cx", split_axis=0, concat_axis=0, tiled=True)
    owners, slots, columns = received.shape
    produced = feed_forward(
        received.reshape(owners * slots, columns), gate_weight, up_weight, down_weight
    )
    returned = lax.all_to_all(
        produced.reshape(owners, slots, columns).astype(jnp.bfloat16),
        "cx",
        split_axis=0,
        concat_axis=0,
        tiled=True,
    ).astype(jnp.float32)
    halves = jnp.sum(returned.reshape(expert_count, 2, capacity, model_width), axis=1)
    moe_rows = jnp.dot(
        weighting,
        halves.reshape(expert_count * capacity, model_width),
        precision=highest_precision,
        preferred_element_type=jnp.float32,
    )
    moe_share = lax.psum_scatter(
        moe_rows.astype(jnp.bfloat16), "tp", scatter_dimension=1, tiled=True
    ).astype(jnp.float32)
    return (hidden_share + moe_share).astype(jnp.bfloat16)


MESH = pl.DeviceIdType.MESH
VMEM_BYTES = 50 * 1024 * 1024
CHIPS = 4
PIECES = 4


def neighbours():
    cx, tp = lax.axis_index("cx"), lax.axis_index("tp")
    sibling = cx + 1 - 2 * (cx % 2)
    along_x = cx + 2 - 4 * ((cx // 2) % 2)
    along_y = (cx + 4) % 8
    return cx, tp, sibling, along_x, along_y


def partners(tp):
    return [tp, tp + 1 - 2 * (tp % 2), (tp + 2) % 4, 3 - tp]


def greet(devices):
    barrier = pltpu.get_barrier_semaphore()
    for device in devices:
        pl.semaphore_signal(barrier, inc=1, device_id=device, device_id_type=MESH)
    pl.semaphore_wait(barrier, len(devices))


class Copies:
    def __init__(self, send, recv):
        self.send, self.recv, self.numbers, self.started = send, recv, {}, []

    def make(self, name, source, target, device):
        number = self.numbers.setdefault(name, len(self.numbers))
        return pltpu.make_async_remote_copy(
            src_ref=source,
            dst_ref=target,
            send_sem=self.send.at[number],
            recv_sem=self.recv.at[number],
            device_id=device,
            device_id_type=MESH,
        )

    def start(self, name, source, target, device):
        copy = self.make(name, source, target, device)
        copy.start()
        self.started.append(copy)

    def wait(self, name, landed, device):
        self.make(name, landed, landed, device).wait_recv()

    def drain(self):
        for copy in self.started:
            copy.wait_send()


def plane_gather(copies, place, rows, split):
    cx, tp, sibling, along_x, along_y = neighbours()
    across = (along_x + 4) % 8
    to_sibling, to_x, to_y = (sibling, tp), (along_x, tp), (along_y, tp)
    parts = ((0, split), (split, rows - split))

    def pair(owner):
        return owner + 1 - 2 * (owner % 2)

    def push(name, owner, piece, part, device):
        ref = place(owner, piece, *part)
        copies.start(name, ref, ref, device)

    def arrive(name, owner, piece, part):
        copies.wait(name, place(owner, piece, *part), to_sibling)

    whole = (0, rows)

    def stage(j, piece):
        push(("x", j), cx, piece, whole, to_x)
        push(("y", j), cx, piece, whole, to_y)
        push(("own", j), cx, piece, whole, to_sibling)

    def forward(j, piece):
        arrive(("x", j), along_x, piece, whole)
        push(("dy", j), along_x, piece, parts[0], to_y)
        push(("sx", j), along_x, piece, whole, to_sibling)
        arrive(("y", j), along_y, piece, whole)
        push(("dx", j), along_y, piece, parts[1], to_x)
        push(("sy", j), along_y, piece, whole, to_sibling)

    def corner(j, piece):
        arrive(("dy", j), across, piece, parts[0])
        push(("sd0", j), across, piece, parts[0], to_sibling)
        arrive(("dx", j), across, piece, parts[1])
        push(("sd1", j), across, piece, parts[1], to_sibling)

    def finish(j, piece, which):
        if which == 0:
            arrive(("own", j), pair(cx), piece, whole)
        if which == 1:
            arrive(("sx", j), pair(along_x), piece, whole)
            arrive(("sy", j), pair(along_y), piece, whole)
        if which == 2:
            arrive(("sd0", j), pair(across), piece, parts[0])
            arrive(("sd1", j), pair(across), piece, parts[1])

    return stage, forward, corner, finish


def state_kernel(rows, split, block_ref, all_ref, last_ref, send, recv, local):
    cx, tp, sibling, along_x, along_y = neighbours()
    own = pltpu.make_async_copy(block_ref, all_ref.at[cx], local)
    own.start()
    greet([(sibling, tp), (along_x, tp), (along_y, tp)])
    own.wait()
    copies = Copies(send, recv)

    def place(owner, piece, first, count):
        return all_ref.at[owner, pl.ds(first, count), :]

    stage, forward, corner, finish = plane_gather(copies, place, rows, split)
    stage(0, 0)
    forward(0, 0)
    corner(0, 0)
    for which in range(3):
        finish(0, 0, which)
    last_ref[...] = all_ref[:, rows - 16 :, :].astype(jnp.float32)
    copies.drain()


def gather_states(block):
    rows = block.shape[0]
    return pl.pallas_call(
        functools.partial(state_kernel, rows, rows // 32 * 16),
        out_shape=(
            jax.ShapeDtypeStruct((2 * CHIPS,) + block.shape, block.dtype),
            jax.ShapeDtypeStruct((2 * CHIPS, 16, block.shape[1]), jnp.float32),
        ),
        in_specs=[pl.BlockSpec(memory_space=pltpu.VMEM)],
        out_specs=(pl.BlockSpec(memory_space=pltpu.VMEM), pl.BlockSpec(memory_space=pltpu.VMEM)),
        scratch_shapes=[
            pltpu.SemaphoreType.DMA((9,)),
            pltpu.SemaphoreType.DMA((9,)),
            pltpu.SemaphoreType.DMA,
        ],
        compiler_params=pltpu.CompilerParams(
            collective_id=1, has_side_effects=True, vmem_limit_bytes=VMEM_BYTES
        ),
        name="gather_states",
    )(block)


def layer_kernel(
    partial_ref,
    layer_ref,
    gain_ref,
    router_ref,
    ids_ref,
    gate_hbm,
    up_hbm,
    down_hbm,
    out_ref,
    hidden_ref,
    all_ref,
    squares,
    gate_ref,
    up_ref,
    down_ref,
    gate_sum,
    up_sum,
    activated,
    produced_ref,
    paired,
    outbox,
    inbox,
    corner_out,
    x_out,
    y_out,
    corner_x,
    corner_y,
    x_in,
    y_in,
    z_out,
    z_in,
    send,
    recv,
    local,
):
    cx, tp, sibling, along_x, along_y = neighbours()
    rows, share = layer_ref.shape
    hidden_units = down_ref.shape[0]
    width = down_ref.shape[1]
    half = rows // 2
    top, low = pl.ds(0, half), pl.ds(half, half)
    peers = partners(tp)
    across = (along_x + 4) % 8
    to_sibling, to_x, to_y = (sibling, tp), (along_x, tp), (along_y, tp)
    loads = [
        pltpu.make_async_copy(source, target, local.at[k])
        for k, (source, target) in enumerate(
            ((gate_hbm, gate_ref), (up_hbm, up_ref), (down_hbm, down_ref))
        )
    ]
    for load in loads:
        load.start()
    greet([to_sibling, to_x, to_y] + [(cx, peer) for peer in peers[1:]])
    copies = Copies(send, recv)

    def columns(piece):
        return pl.ds(pl.multiple_of(piece * share, share), share)

    outbox[3] = partial_ref[:, columns(peers[3])].astype(jnp.bfloat16)
    copies.start(("sum", 3), outbox.at[3], inbox.at[2], (cx, peers[1]))
    outbox[1] = partial_ref[:, columns(peers[1])].astype(jnp.bfloat16)
    copies.start(("sum", 1), outbox.at[1], inbox.at[1], (cx, peers[1]))
    hidden = partial_ref[:, columns(tp)] + layer_ref[...].astype(jnp.float32)
    copies.wait(("sum", 3), inbox.at[2], (cx, peers[1]))
    outbox[2] = (partial_ref[:, columns(peers[2])] + inbox[2].astype(jnp.float32)).astype(
        jnp.bfloat16
    )
    copies.start(("sum", 2), outbox.at[2], inbox.at[3], (cx, peers[2]))
    copies.wait(("sum", 1), inbox.at[1], (cx, peers[1]))
    hidden = hidden + inbox[1].astype(jnp.float32)
    copies.wait(("sum", 2), inbox.at[3], (cx, peers[2]))
    hidden = hidden + inbox[3].astype(jnp.float32)
    hidden_ref[...] = hidden
    squares[0] = lax.dot_general(
        jnp.ones((8, share), jnp.float32),
        hidden * hidden,
        (((1,), (1,)), ((), ())),
        precision=highest_precision,
        preferred_element_type=jnp.float32,
    )
    for j in (3, 2, 1):
        copies.start(("squares", j), squares.at[0], squares.at[j], (cx, peers[j]))
    total = squares[0]
    for j in (1, 2, 3):
        copies.wait(("squares", j), squares.at[j], (cx, peers[j]))
        total = total + squares[j]
    scale = lax.rsqrt(total / (share * PIECES) + epsilon)
    scale = jnp.transpose(jnp.broadcast_to(scale[0:1, :], (rows, rows)))[:, 0:1]
    first_row = pl.multiple_of(cx * rows, rows)
    all_ref[pl.ds(first_row, rows), columns(tp)] = (
        hidden_ref[...] * scale * gain_ref[:, columns(tp)]
    ).astype(jnp.bfloat16)

    def place(owner, piece, start, count):
        return all_ref.at[
            pl.ds(pl.multiple_of(owner * rows + start, 16), count), columns(piece)
        ]

    stage, forward, corner, finish = plane_gather(copies, place, rows, half)
    mine = place(cx, tp, 0, rows)
    for j in (2, 1):
        copies.start(("z", j), mine, mine, (cx, peers[j]))
    stage(0, peers[0])

    def take(j):
        landed = place(cx, peers[j], 0, rows)
        copies.wait(("z", j), landed, (cx, peers[j]))
        if j == 2:
            copies.start(("z", 3), landed, landed, (cx, peers[1]))
        stage(j, peers[j])

    expert = (cx // 2).astype(jnp.float32)
    expert_count = router_ref.shape[1]

    def choice(owner):
        first, second = [
            jnp.transpose(jnp.broadcast_to(ids_ref[owner, k : k + 1, :], (rows, rows)))[
                :, :expert_count
            ]
            for k in range(2)
        ]
        lanes = lax.broadcasted_iota(jnp.int32, (rows, expert_count), 1).astype(jnp.float32)

        def equal(a, b):
            return jnp.where(a == b, 1.0, 0.0)

        return (equal(first, lanes) - equal(second, lanes)) * (
            equal(first, expert) - equal(second, expert)
        )

    def chip_rows(owner):
        return pl.ds(pl.multiple_of(owner // 2 * (2 * rows), 2 * rows), 2 * rows)

    def lift(owner, piece=None, slot=0, opening=True, closing=True):
        here = chip_rows(owner)
        depth = pl.ds(0, width) if piece is None else columns(piece)

        def step(n, carry):
            units = pl.ds(pl.multiple_of(n * 256, 256), 256)
            block = all_ref[here, depth]
            gated = jnp.dot(block, gate_ref[depth, units], preferred_element_type=jnp.float32)
            lifted = jnp.dot(block, up_ref[depth, units], preferred_element_type=jnp.float32)
            if not opening:
                gated = gated + gate_sum[slot, :, units]
                lifted = lifted + up_sum[slot, :, units]
            if closing:
                activated[:, units] = (gated * jax.nn.sigmoid(gated) * lifted).astype(jnp.bfloat16)
            else:
                gate_sum[slot, :, units] = gated
                up_sum[slot, :, units] = lifted
            return carry

        lax.fori_loop(0, hidden_units // 256, step, 0)

    def lower(k):
        owner = homes[k]
        here = chip_rows(owner)
        first = owner - owner % 2
        logits = jnp.dot(all_ref[here], router_ref[...], preferred_element_type=jnp.float32)
        select = jnp.concatenate([choice(first), choice(first + 1)])
        weight = jax.nn.sigmoid(jnp.sum(logits * select, axis=1, keepdims=True))
        weight = weight * (0.5 * jnp.sum(select * select, axis=1, keepdims=True))
        other = owner + 1 - 2 * (owner % 2)
        for j in order:
            product = jnp.dot(
                activated[...], down_ref[:, columns(peers[j])], preferred_element_type=jnp.float32
            )
            produced_ref[here, columns(peers[j])] = (product * weight).astype(jnp.bfloat16)
            copies.start(("pair", j, k), part(other, j), paired.at[j, k], to_sibling)

    homes = (across, along_x, along_y, cx)
    order = (3, 2, 1, 0)

    def part(owner, j):
        return produced_ref.at[
            pl.ds(pl.multiple_of(owner * rows, rows), rows), columns(peers[j])
        ]

    def both(j, k):
        copies.wait(("pair", j, k), paired.at[j, k], to_sibling)
        return part(homes[k], j)[...].astype(jnp.float32) + paired[j, k].astype(jnp.float32)

    def send_x(j):
        x_out[j] = both(j, 1).astype(jnp.bfloat16)
        copies.start(("x0", j), x_out.at[j, top], x_in.at[j, top], to_x)

    def send_y(j):
        y_out[j] = both(j, 2).astype(jnp.bfloat16)
        copies.start(("y1", j), y_out.at[j, low], y_in.at[j, low], to_y)

    def send_corner(j):
        corner_out[j] = both(j, 0).astype(jnp.bfloat16)
        copies.start(("cx", j), corner_out.at[j, top], corner_x.at[j], to_x)
        copies.start(("cy", j), corner_out.at[j, low], corner_y.at[j], to_y)

    def second(j):
        copies.wait(("cx", j), corner_x.at[j], to_x)
        y_out[j, top] = (
            y_out[j, top].astype(jnp.float32) + corner_x[j].astype(jnp.float32)
        ).astype(jnp.bfloat16)
        copies.start(("y0", j), y_out.at[j, top], y_in.at[j, top], to_y)
        copies.wait(("cy", j), corner_y.at[j], to_y)
        x_out[j, low] = (
            x_out[j, low].astype(jnp.float32) + corner_y[j].astype(jnp.float32)
        ).astype(jnp.bfloat16)
        copies.start(("x1", j), x_out.at[j, low], x_in.at[j, low], to_x)

    def third(j):
        total = both(j, 3)
        copies.wait(("x0", j), x_in.at[j, top], to_x)
        copies.wait(("y1", j), y_in.at[j, low], to_y)
        copies.wait(("y0", j), y_in.at[j, top], to_y)
        copies.wait(("x1", j), x_in.at[j, low], to_x)
        total = total + x_in[j].astype(jnp.float32) + y_in[j].astype(jnp.float32)
        if j == 2:
            copies.wait(("z_out", 3), z_in.at[2], (cx, peers[1]))
            total = total + z_in[2].astype(jnp.float32)
        if j:
            slot, peer = {3: (2, 1), 2: (3, 2), 1: (1, 1)}[j]
            z_out[j] = total.astype(jnp.bfloat16)
            copies.start(("z_out", j), z_out.at[j], z_in.at[slot], (cx, peers[peer]))
        return total

    def lift_sides(j):
        finish(j, peers[j], 1)
        for slot, owner in enumerate((along_x, along_y)):
            lift(owner, peers[j], slot, opening=j == 0, closing=False)

    take(1)
    forward(0, peers[0])
    take(2)
    forward(1, peers[1])
    corner(0, peers[0])
    for load in loads:
        load.wait()
    lift_sides(0)
    take(3)
    forward(2, peers[2])
    corner(1, peers[1])
    lift_sides(1)
    forward(3, peers[3])
    corner(2, peers[2])
    lift_sides(2)
    finish(3, peers[3], 1)
    lift(along_x, peers[3], 0, opening=False)
    lower(1)
    corner(3, peers[3])
    lift(along_y, peers[3], 1, opening=False)
    lower(2)
    for j in order:
        send_x(j)
    for j in range(PIECES):
        finish(j, peers[j], 2)
    lift(across)
    lower(0)
    for j in order:
        send_y(j)
    for j in order:
        send_corner(j)
    for j in range(PIECES):
        finish(j, peers[j], 0)
    lift(cx)
    second(3)
    second(2)
    lower(3)
    third(3)
    second(1)
    second(0)
    third(2)
    third(1)
    total = third(0) + hidden_ref[...]
    copies.wait(("z_out", 1), z_in.at[1], (cx, peers[1]))
    copies.wait(("z_out", 2), z_in.at[3], (cx, peers[2]))
    total = total + z_in[1].astype(jnp.float32) + z_in[3].astype(jnp.float32)
    out_ref[...] = total.astype(jnp.bfloat16)
    copies.drain()


def experts_layer(partial_rows, layer_input, gain, router, ids, w_gate, w_up, w_down):
    rows, share = layer_input.shape
    width, units = w_gate.shape
    everyone = 2 * CHIPS * rows
    in_vmem = pl.BlockSpec(memory_space=pltpu.VMEM)
    anywhere = pl.BlockSpec(memory_space=pl.ANY)
    piece = pltpu.VMEM((PIECES, rows, share), jnp.bfloat16)
    half = pltpu.VMEM((PIECES, rows // 2, share), jnp.bfloat16)
    work = everyone * 6 * width * units
    return pl.pallas_call(
        layer_kernel,
        out_shape=jax.ShapeDtypeStruct((rows, share), jnp.bfloat16),
        in_specs=[in_vmem] * 5 + [anywhere] * 3,
        out_specs=in_vmem,
        scratch_shapes=[
            pltpu.VMEM((rows, share), jnp.float32),
            pltpu.VMEM((everyone, width), jnp.bfloat16),
            pltpu.VMEM((PIECES, 8, rows), jnp.float32),
            pltpu.VMEM((width, units), jnp.bfloat16),
            pltpu.VMEM((width, units), jnp.bfloat16),
            pltpu.VMEM((units, width), jnp.bfloat16),
            pltpu.VMEM((2, 2 * rows, units), jnp.float32),
            pltpu.VMEM((2, 2 * rows, units), jnp.float32),
            pltpu.VMEM((2 * rows, units), jnp.bfloat16),
            pltpu.VMEM((everyone, width), jnp.bfloat16),
            pltpu.VMEM((PIECES, CHIPS, rows, share), jnp.bfloat16),
        ]
        + [piece] * 5
        + [half] * 2
        + [piece] * 4
        + [pltpu.SemaphoreType.DMA((88,)), pltpu.SemaphoreType.DMA((88,))]
        + [pltpu.SemaphoreType.DMA((3,))],
        compiler_params=pltpu.CompilerParams(
            collective_id=2, has_side_effects=True, vmem_limit_bytes=VMEM_BYTES
        ),
        cost_estimate=pl.CostEstimate(
            flops=work, bytes_accessed=6 * width * units, transcendentals=0
        ),
        name="experts_layer",
    )(partial_rows, layer_input, gain, router, ids, w_gate, w_up, w_down)


def shards_dense(
    layer_input,
    queries,
    keys,
    values,
    gate_input,
    log_decay,
    prior_state,
    attn_gain,
    out_weight,
    moe_gain,
    router,
    expert_ids,
    w_gate,
    w_up,
    w_down,
):
    positions = queries.shape[0]
    heads_here = log_decay.shape[0]
    head_size = prior_state.shape[1]
    me = lax.axis_index("cx")
    query_vectors = queries.reshape(positions, heads_here, head_size)
    key_rows = keys.reshape(positions, heads_here, head_size)
    value_single_float = values.reshape(positions, heads_here, head_size).astype(jnp.float32)
    running_state = jnp.cumsum(log_decay, axis=1)
    trailing_rows = jnp.exp(running_state[:, -1:] - running_state)
    key_single_float = key_rows.astype(jnp.float32) * trailing_rows.T[:, :, None]
    within_block_state = jnp.einsum(
        "gpc,gpw->pcw", key_single_float, value_single_float, precision=highest_precision
    )
    total_decay = running_state[:, -1]
    coarse = lax.reduce_precision(total_decay, 8, 7)
    decay_row = jnp.concatenate(
        [coarse, total_decay - coarse, jnp.zeros((head_size - 2 * heads_here,), jnp.float32)]
    )
    extra = jnp.concatenate(
        [
            expert_ids.T.astype(jnp.float32),
            decay_row[None, :],
            jnp.zeros((13, head_size), jnp.float32),
        ]
    )
    state_rows = heads_here * head_size
    block = jnp.concatenate(
        [within_block_state.reshape(state_rows, head_size), extra]
    ).astype(jnp.bfloat16)
    gathered, all_ids = gather_states(block)
    decays = all_ids[:, 2, :]
    decays = decays[:, :heads_here] + decays[:, heads_here : 2 * heads_here]
    peers = decays.shape[0]
    spot = jnp.arange(peers)
    earlier = spot < me
    decays = jnp.where(earlier[:, None], decays, 0.0)
    later = spot[None, :] > spot[:, None]
    factor = jnp.exp(jnp.sum(jnp.where(later[:, :, None], decays[None], 0.0), axis=1))
    factor = jnp.where(earlier[:, None], factor, 0.0)
    all_states = gathered[:, :state_rows, :].reshape(peers, heads_here, head_size, head_size)
    incoming_state = jnp.exp(jnp.sum(decays, axis=0))[:, None, None] * prior_state + jnp.sum(
        factor[:, :, None, None] * all_states.astype(jnp.float32), axis=0
    )
    causal = (jnp.arange(positions)[:, None] >= jnp.arange(positions)[None, :])[None]
    spread = running_state[:, :, None] - running_state[:, None, :]
    weights = jnp.where(causal, jnp.exp(jnp.where(causal, spread, 0.0)), 0.0)
    scores = (
        jnp.einsum("thk,shk->hts", query_vectors, key_rows, preferred_element_type=jnp.float32)
        * weights
    )
    inner = jnp.einsum("hts,shv->thv", scores, value_single_float, precision=highest_precision)
    carried_contribution = jnp.exp(running_state).T[:, :, None] * jnp.einsum(
        "rxg,xgd->rxd",
        query_vectors.astype(jnp.float32),
        incoming_state,
        precision=highest_precision,
    )
    attended = inner + carried_contribution
    squares = jnp.mean(attended * attended, axis=-1, keepdims=True)
    gating = jax.nn.sigmoid(
        gate_input.astype(jnp.float32).reshape(positions, heads_here, head_size)
    )
    normed = (
        attended * lax.rsqrt(squares + epsilon) * attn_gain.reshape(heads_here, head_size) * gating
    )
    normed = normed.astype(jnp.bfloat16).reshape(positions, heads_here * head_size)
    partial_rows = jnp.dot(normed, out_weight, preferred_element_type=jnp.float32)
    return experts_layer(
        partial_rows, layer_input, moe_gain[None, :], router, all_ids, w_gate[0], w_up[0], w_down[0]
    )


def solution(mesh):
    placed = (
        P("cx", "tp"),
        P("cx", "tp"),
        P("cx", "tp"),
        P("cx", "tp"),
        P("cx", "tp"),
        P("tp", "cx"),
        P("tp", None, None),
        P("tp"),
        P("tp", None),
        P(),
        P(),
        P("cx", None),
        P("cx", None, "tp"),
        P("cx", None, "tp"),
        P("cx", "tp", None),
    )
    dense = mesh.shape["cx"] == 2 * CHIPS and mesh.shape["tp"] == PIECES
    shards = shards_dense if dense else shards_routed
    return jax.shard_map(
        shards, mesh=mesh, in_specs=placed, out_specs=P("cx", "tp"), check_vma=False
    )
```

```python
import functools

import jax
import jax.numpy as jnp
from jax import lax
from jax.experimental import pallas as pl
from jax.experimental.pallas import tpu as pltpu
from jax.sharding import PartitionSpec as P

epsilon = 1e-06
highest_precision = lax.Precision.HIGHEST


def prefix(shard, axis, combine, identity):
    peers, index = (lax.axis_size(axis), lax.axis_index(axis))
    everything = jax.tree.map(lambda part: lax.all_gather(part, axis), shard)
    start = jax.tree.map(
        lambda part, zero: jnp.broadcast_to(jnp.asarray(zero, part.dtype), part.shape),
        shard,
        identity,
    )

    def lap(k, before):
        reached = k < index
        new = combine(before, jax.tree.map(lambda part: part[k], everything))
        return jax.tree.map(lambda a, b: jnp.where(reached, a, b), new, before)

    return lax.fori_loop(0, peers, lap, start)


def feed_forward(routed, gate_weight, up_weight, down_weight):
    gated = jnp.dot(routed, gate_weight, preferred_element_type=jnp.float32)
    lifted = jnp.dot(routed, up_weight, preferred_element_type=jnp.float32)
    activated = (jax.nn.silu(gated) * lifted).astype(jnp.bfloat16)
    return jnp.dot(activated, down_weight, preferred_element_type=jnp.float32)


def combine_states(earlier, later):
    return (earlier[0] + later[0], jnp.exp(later[0])[:, None, None] * earlier[1] + later[1])


def shards_routed(
    layer_input,
    queries,
    keys,
    values,
    gate_input,
    log_decay,
    prior_state,
    attn_gain,
    out_weight,
    moe_gain,
    router,
    expert_ids,
    w_gate,
    w_up,
    w_down,
):
    positions = queries.shape[0]
    heads_here = log_decay.shape[0]
    head_size = prior_state.shape[1]
    query_vectors = queries.reshape(positions, heads_here, head_size)
    key_rows = keys.reshape(positions, heads_here, head_size)
    value_single_float = values.reshape(positions, heads_here, head_size).astype(jnp.float32)
    running_state = jnp.cumsum(log_decay, axis=1)
    causal = (jnp.arange(positions)[:, None] >= jnp.arange(positions)[None, :])[None]
    spread = running_state[:, :, None] - running_state[:, None, :]
    weights = jnp.where(causal, jnp.exp(jnp.where(causal, spread, 0.0)), 0.0)
    scores = (
        jnp.einsum("thk,shk->hts", query_vectors, key_rows, preferred_element_type=jnp.float32)
        * weights
    )
    inner = jnp.einsum("hts,shv->thv", scores, value_single_float, precision=highest_precision)
    trailing_rows = jnp.exp(running_state[:, -1:] - running_state)
    key_single_float = key_rows.astype(jnp.float32) * trailing_rows.T[:, :, None]
    within_block_state = jnp.einsum(
        "gpc,gpw->pcw", key_single_float, value_single_float, precision=highest_precision
    )
    total_decay = running_state[:, -1]
    identity = (
        jnp.zeros((heads_here,), jnp.float32),
        jnp.zeros((heads_here, head_size, head_size), jnp.float32),
    )
    before_total, before_state = prefix(
        (total_decay, within_block_state), "cx", combine_states, identity
    )
    incoming_state = jnp.exp(before_total)[:, None, None] * prior_state + before_state
    carried_contribution = jnp.exp(running_state).T[:, :, None] * jnp.einsum(
        "rxg,xgd->rxd",
        query_vectors.astype(jnp.float32),
        incoming_state,
        precision=highest_precision,
    )
    attended = inner + carried_contribution
    squares = jnp.mean(attended * attended, axis=-1, keepdims=True)
    gating = jax.nn.sigmoid(
        gate_input.astype(jnp.float32).reshape(positions, heads_here, head_size)
    )
    normed = (
        attended * lax.rsqrt(squares + epsilon) * attn_gain.reshape(heads_here, head_size) * gating
    )
    normed = normed.astype(jnp.bfloat16).reshape(positions, heads_here * head_size)
    partial_rows = jnp.dot(normed, out_weight, preferred_element_type=jnp.float32)
    model_width = out_weight.shape[1]
    width_share = layer_input.shape[1]
    column_start = lax.axis_index("tp") * width_share
    own_columns = lax.dynamic_slice_in_dim(
        partial_rows, column_start, width_share, 1
    ) + layer_input.astype(jnp.float32)
    partial_rows = lax.dynamic_update_slice_in_dim(partial_rows, own_columns, column_start, 1)
    expert_count = router.shape[1]
    hidden_state = lax.psum(partial_rows, "tp")
    row_mean = jnp.mean(hidden_state * hidden_state, axis=-1, keepdims=True)
    full_input = (hidden_state * lax.rsqrt(row_mean + epsilon) * moe_gain).astype(jnp.bfloat16)
    logits = jnp.dot(full_input, router, preferred_element_type=jnp.float32)
    hidden_share = lax.dynamic_slice_in_dim(hidden_state, column_start, width_share, 1)
    matched = expert_ids[:, :, None] == jnp.arange(expert_count, dtype=jnp.int32)[None, None, :]
    chosen = jnp.sum(jnp.where(matched, logits[:, None, :], 0.0), axis=-1)
    margin = chosen[:, 0] - chosen[:, 1]
    mixing = jnp.stack([jax.nn.sigmoid(margin), jax.nn.sigmoid(-margin)], axis=1)
    choices_made = expert_ids.shape[1]
    onehot = matched.reshape(positions * choices_made, expert_count).astype(jnp.int32)
    before = jnp.cumsum(onehot, axis=0) - onehot
    position = jnp.sum(before * onehot, axis=1).reshape(positions, choices_made)
    capacity = 8 * positions // lax.axis_size("cx")
    at_slot = position[:, :, None] == jnp.arange(capacity, dtype=jnp.int32)[None, None, :]
    picked = matched[:, :, :, None] & at_slot[:, :, None, :]
    dispatch = (
        jnp.sum(picked, axis=1).astype(jnp.bfloat16).reshape(positions, expert_count * capacity)
    )
    weighting = jnp.sum(jnp.where(picked, mixing[:, :, None, None], 0.0), axis=1).reshape(
        positions, expert_count * capacity
    )
    gate_weight = w_gate[0]
    up_weight = w_up[0]
    down_weight = w_down[0]
    outgoing = jnp.einsum(
        "tm,td->md", dispatch, full_input, preferred_element_type=jnp.float32
    ).astype(jnp.bfloat16)
    outgoing = jnp.repeat(outgoing.reshape(expert_count, capacity, model_width), 2, axis=0)
    received = lax.all_to_all(outgoing, "cx", split_axis=0, concat_axis=0, tiled=True)
    owners, slots, columns = received.shape
    produced = feed_forward(
        received.reshape(owners * slots, columns), gate_weight, up_weight, down_weight
    )
    returned = lax.all_to_all(
        produced.reshape(owners, slots, columns).astype(jnp.bfloat16),
        "cx",
        split_axis=0,
        concat_axis=0,
        tiled=True,
    ).astype(jnp.float32)
    halves = jnp.sum(returned.reshape(expert_count, 2, capacity, model_width), axis=1)
    moe_rows = jnp.dot(
        weighting,
        halves.reshape(expert_count * capacity, model_width),
        precision=highest_precision,
        preferred_element_type=jnp.float32,
    )
    moe_share = lax.psum_scatter(
        moe_rows.astype(jnp.bfloat16), "tp", scatter_dimension=1, tiled=True
    ).astype(jnp.float32)
    return (hidden_share + moe_share).astype(jnp.bfloat16)


MESH = pl.DeviceIdType.MESH
VMEM_BYTES = 50 * 1024 * 1024
CHIPS = 4
PIECES = 4


def neighbours():
    cx, tp = lax.axis_index("cx"), lax.axis_index("tp")
    sibling = cx + 1 - 2 * (cx % 2)
    along_x = cx + 2 - 4 * ((cx // 2) % 2)
    along_y = (cx + 4) % 8
    return cx, tp, sibling, along_x, along_y


def partners(tp):
    return [tp, tp + 1 - 2 * (tp % 2), (tp + 2) % 4, 3 - tp]


def greet(devices):
    barrier = pltpu.get_barrier_semaphore()
    for device in devices:
        pl.semaphore_signal(barrier, inc=1, device_id=device, device_id_type=MESH)
    pl.semaphore_wait(barrier, len(devices))


class Copies:
    def __init__(self, send, recv):
        self.send, self.recv, self.numbers, self.started = send, recv, {}, []

    def make(self, name, source, target, device):
        number = self.numbers.setdefault(name, len(self.numbers))
        return pltpu.make_async_remote_copy(
            src_ref=source,
            dst_ref=target,
            send_sem=self.send.at[number],
            recv_sem=self.recv.at[number],
            device_id=device,
            device_id_type=MESH,
        )

    def start(self, name, source, target, device):
        copy = self.make(name, source, target, device)
        copy.start()
        self.started.append(copy)

    def wait(self, name, landed, device):
        self.make(name, landed, landed, device).wait_recv()

    def drain(self):
        for copy in self.started:
            copy.wait_send()


def plane_gather(copies, place, rows, split):
    cx, tp, sibling, along_x, along_y = neighbours()
    across = (along_x + 4) % 8
    to_sibling, to_x, to_y = (sibling, tp), (along_x, tp), (along_y, tp)
    parts = ((0, split), (split, rows - split))

    def pair(owner):
        return owner + 1 - 2 * (owner % 2)

    def push(name, owner, piece, part, device):
        ref = place(owner, piece, *part)
        copies.start(name, ref, ref, device)

    def arrive(name, owner, piece, part):
        copies.wait(name, place(owner, piece, *part), to_sibling)

    whole = (0, rows)

    def stage(j, piece):
        push(("x", j), cx, piece, whole, to_x)
        push(("y", j), cx, piece, whole, to_y)
        push(("own", j), cx, piece, whole, to_sibling)

    def forward(j, piece):
        arrive(("x", j), along_x, piece, whole)
        push(("dy", j), along_x, piece, parts[0], to_y)
        push(("sx", j), along_x, piece, whole, to_sibling)
        arrive(("y", j), along_y, piece, whole)
        push(("dx", j), along_y, piece, parts[1], to_x)
        push(("sy", j), along_y, piece, whole, to_sibling)

    def corner(j, piece):
        arrive(("dy", j), across, piece, parts[0])
        push(("sd0", j), across, piece, parts[0], to_sibling)
        arrive(("dx", j), across, piece, parts[1])
        push(("sd1", j), across, piece, parts[1], to_sibling)

    def finish(j, piece, which):
        if which == 0:
            arrive(("own", j), pair(cx), piece, whole)
        if which == 1:
            arrive(("sx", j), pair(along_x), piece, whole)
            arrive(("sy", j), pair(along_y), piece, whole)
        if which == 2:
            arrive(("sd0", j), pair(across), piece, parts[0])
            arrive(("sd1", j), pair(across), piece, parts[1])

    return stage, forward, corner, finish


def state_kernel(rows, split, block_ref, all_ref, last_ref, send, recv, local):
    cx, tp, sibling, along_x, along_y = neighbours()
    own = pltpu.make_async_copy(block_ref, all_ref.at[cx], local)
    own.start()
    greet([(sibling, tp), (along_x, tp), (along_y, tp)])
    own.wait()
    copies = Copies(send, recv)

    def place(owner, piece, first, count):
        return all_ref.at[owner, pl.ds(first, count), :]

    stage, forward, corner, finish = plane_gather(copies, place, rows, split)
    stage(0, 0)
    forward(0, 0)
    corner(0, 0)
    for which in range(3):
        finish(0, 0, which)
    last_ref[...] = all_ref[:, rows - 16 :, :].astype(jnp.float32)
    copies.drain()


def gather_states(block):
    rows = block.shape[0]
    return pl.pallas_call(
        functools.partial(state_kernel, rows, rows // 32 * 16),
        out_shape=(
            jax.ShapeDtypeStruct((2 * CHIPS,) + block.shape, block.dtype),
            jax.ShapeDtypeStruct((2 * CHIPS, 16, block.shape[1]), jnp.float32),
        ),
        in_specs=[pl.BlockSpec(memory_space=pltpu.VMEM)],
        out_specs=(pl.BlockSpec(memory_space=pltpu.VMEM), pl.BlockSpec(memory_space=pltpu.VMEM)),
        scratch_shapes=[
            pltpu.SemaphoreType.DMA((9,)),
            pltpu.SemaphoreType.DMA((9,)),
            pltpu.SemaphoreType.DMA,
        ],
        compiler_params=pltpu.CompilerParams(
            collective_id=1, has_side_effects=True, vmem_limit_bytes=VMEM_BYTES
        ),
        name="gather_states",
    )(block)


def layer_kernel(
    partial_ref,
    layer_ref,
    gain_ref,
    router_ref,
    ids_ref,
    gate_hbm,
    up_hbm,
    down_hbm,
    out_ref,
    hidden_ref,
    all_ref,
    squares,
    gate_ref,
    up_ref,
    down_ref,
    gate_sum,
    up_sum,
    activated,
    produced_ref,
    paired,
    outbox,
    inbox,
    corner_out,
    x_out,
    y_out,
    corner_x,
    corner_y,
    x_in,
    y_in,
    z_out,
    z_in,
    send,
    recv,
    local,
):
    cx, tp, sibling, along_x, along_y = neighbours()
    rows, share = layer_ref.shape
    hidden_units = down_ref.shape[0]
    width = down_ref.shape[1]
    half = rows // 2
    top, low = pl.ds(0, half), pl.ds(half, half)
    peers = partners(tp)
    across = (along_x + 4) % 8
    to_sibling, to_x, to_y = (sibling, tp), (along_x, tp), (along_y, tp)
    loads = [
        pltpu.make_async_copy(source, target, local.at[k])
        for k, (source, target) in enumerate(
            ((gate_hbm, gate_ref), (up_hbm, up_ref), (down_hbm, down_ref))
        )
    ]
    for load in loads:
        load.start()
    greet([to_sibling, to_x, to_y] + [(cx, peer) for peer in peers[1:]])
    copies = Copies(send, recv)

    def columns(piece):
        return pl.ds(pl.multiple_of(piece * share, share), share)

    outbox[3] = partial_ref[:, columns(peers[3])].astype(jnp.bfloat16)
    copies.start(("sum", 3), outbox.at[3], inbox.at[2], (cx, peers[1]))
    outbox[1] = partial_ref[:, columns(peers[1])].astype(jnp.bfloat16)
    copies.start(("sum", 1), outbox.at[1], inbox.at[1], (cx, peers[1]))
    hidden = partial_ref[:, columns(tp)] + layer_ref[...].astype(jnp.float32)
    copies.wait(("sum", 3), inbox.at[2], (cx, peers[1]))
    outbox[2] = (partial_ref[:, columns(peers[2])] + inbox[2].astype(jnp.float32)).astype(
        jnp.bfloat16
    )
    copies.start(("sum", 2), outbox.at[2], inbox.at[3], (cx, peers[2]))
    copies.wait(("sum", 1), inbox.at[1], (cx, peers[1]))
    hidden = hidden + inbox[1].astype(jnp.float32)
    copies.wait(("sum", 2), inbox.at[3], (cx, peers[2]))
    hidden = hidden + inbox[3].astype(jnp.float32)
    hidden_ref[...] = hidden
    squares[0] = lax.dot_general(
        jnp.ones((8, share), jnp.float32),
        hidden * hidden,
        (((1,), (1,)), ((), ())),
        precision=highest_precision,
        preferred_element_type=jnp.float32,
    )
    for j in (3, 2, 1):
        copies.start(("squares", j), squares.at[0], squares.at[j], (cx, peers[j]))
    total = squares[0]
    for j in (1, 2, 3):
        copies.wait(("squares", j), squares.at[j], (cx, peers[j]))
        total = total + squares[j]
    scale = lax.rsqrt(total / (share * PIECES) + epsilon)
    scale = jnp.transpose(jnp.broadcast_to(scale[0:1, :], (rows, rows)))[:, 0:1]
    first_row = pl.multiple_of(cx * rows, rows)
    all_ref[pl.ds(first_row, rows), columns(tp)] = (
        hidden_ref[...] * scale * gain_ref[:, columns(tp)]
    ).astype(jnp.bfloat16)

    def place(owner, piece, start, count):
        return all_ref.at[
            pl.ds(pl.multiple_of(owner * rows + start, 16), count), columns(piece)
        ]

    stage, forward, corner, finish = plane_gather(copies, place, rows, half)
    mine = place(cx, tp, 0, rows)
    for j in (2, 1):
        copies.start(("z", j), mine, mine, (cx, peers[j]))
    stage(0, peers[0])

    def take(j):
        landed = place(cx, peers[j], 0, rows)
        copies.wait(("z", j), landed, (cx, peers[j]))
        if j == 2:
            copies.start(("z", 3), landed, landed, (cx, peers[1]))
        stage(j, peers[j])

    expert = (cx // 2).astype(jnp.float32)
    expert_count = router_ref.shape[1]

    def choice(owner):
        first, second = [
            jnp.transpose(jnp.broadcast_to(ids_ref[owner, k : k + 1, :], (rows, rows)))[
                :, :expert_count
            ]
            for k in range(2)
        ]
        lanes = lax.broadcasted_iota(jnp.int32, (rows, expert_count), 1).astype(jnp.float32)

        def equal(a, b):
            return jnp.where(a == b, 1.0, 0.0)

        return (equal(first, lanes) - equal(second, lanes)) * (
            equal(first, expert) - equal(second, expert)
        )

    def chip_rows(owner):
        return pl.ds(pl.multiple_of(owner // 2 * (2 * rows), 2 * rows), 2 * rows)

    def lift(owner, piece=None, slot=0, opening=True, closing=True):
        here = chip_rows(owner)
        depth = pl.ds(0, width) if piece is None else columns(piece)

        def step(n, carry):
            units = pl.ds(pl.multiple_of(n * 256, 256), 256)
            block = all_ref[here, depth]
            gated = jnp.dot(block, gate_ref[depth, units], preferred_element_type=jnp.float32)
            lifted = jnp.dot(block, up_ref[depth, units], preferred_element_type=jnp.float32)
            if not opening:
                gated = gated + gate_sum[slot, :, units]
                lifted = lifted + up_sum[slot, :, units]
            if closing:
                activated[:, units] = (gated * jax.nn.sigmoid(gated) * lifted).astype(jnp.bfloat16)
            else:
                gate_sum[slot, :, units] = gated
                up_sum[slot, :, units] = lifted
            return carry

        lax.fori_loop(0, hidden_units // 256, step, 0)

    def lower(k):
        owner = homes[k]
        here = chip_rows(owner)
        first = owner - owner % 2
        logits = jnp.dot(all_ref[here], router_ref[...], preferred_element_type=jnp.float32)
        select = jnp.concatenate([choice(first), choice(first + 1)])
        weight = jax.nn.sigmoid(jnp.sum(logits * select, axis=1, keepdims=True))
        weight = weight * (0.5 * jnp.sum(select * select, axis=1, keepdims=True))
        other = owner + 1 - 2 * (owner % 2)
        for j in order:
            product = jnp.dot(
                activated[...], down_ref[:, columns(peers[j])], preferred_element_type=jnp.float32
            )
            produced_ref[here, columns(peers[j])] = (product * weight).astype(jnp.bfloat16)
            copies.start(("pair", j, k), part(other, j), paired.at[j, k], to_sibling)

    homes = (across, along_x, along_y, cx)
    order = (3, 2, 1, 0)

    def part(owner, j):
        return produced_ref.at[
            pl.ds(pl.multiple_of(owner * rows, rows), rows), columns(peers[j])
        ]

    def both(j, k):
        copies.wait(("pair", j, k), paired.at[j, k], to_sibling)
        return part(homes[k], j)[...].astype(jnp.float32) + paired[j, k].astype(jnp.float32)

    def send_x(j):
        x_out[j] = both(j, 1).astype(jnp.bfloat16)
        copies.start(("x0", j), x_out.at[j, top], x_in.at[j, top], to_x)

    def send_y(j):
        y_out[j] = both(j, 2).astype(jnp.bfloat16)
        copies.start(("y1", j), y_out.at[j, low], y_in.at[j, low], to_y)

    def send_corner(j):
        corner_out[j] = both(j, 0).astype(jnp.bfloat16)
        copies.start(("cx", j), corner_out.at[j, top], corner_x.at[j], to_x)
        copies.start(("cy", j), corner_out.at[j, low], corner_y.at[j], to_y)

    def second(j):
        copies.wait(("cx", j), corner_x.at[j], to_x)
        y_out[j, top] = (
            y_out[j, top].astype(jnp.float32) + corner_x[j].astype(jnp.float32)
        ).astype(jnp.bfloat16)
        copies.start(("y0", j), y_out.at[j, top], y_in.at[j, top], to_y)
        copies.wait(("cy", j), corner_y.at[j], to_y)
        x_out[j, low] = (
            x_out[j, low].astype(jnp.float32) + corner_y[j].astype(jnp.float32)
        ).astype(jnp.bfloat16)
        copies.start(("x1", j), x_out.at[j, low], x_in.at[j, low], to_x)

    def third(j):
        total = both(j, 3)
        copies.wait(("x0", j), x_in.at[j, top], to_x)
        copies.wait(("y1", j), y_in.at[j, low], to_y)
        copies.wait(("y0", j), y_in.at[j, top], to_y)
        copies.wait(("x1", j), x_in.at[j, low], to_x)
        total = total + x_in[j].astype(jnp.float32) + y_in[j].astype(jnp.float32)
        if j == 2:
            copies.wait(("z_out", 3), z_in.at[2], (cx, peers[1]))
            total = total + z_in[2].astype(jnp.float32)
        if j:
            slot, peer = {3: (2, 1), 2: (3, 2), 1: (1, 1)}[j]
            z_out[j] = total.astype(jnp.bfloat16)
            copies.start(("z_out", j), z_out.at[j], z_in.at[slot], (cx, peers[peer]))
        return total

    def lift_sides(j):
        finish(j, peers[j], 1)
        for slot, owner in enumerate((along_x, along_y)):
            lift(owner, peers[j], slot, opening=j == 0, closing=False)

    take(1)
    forward(0, peers[0])
    take(2)
    forward(1, peers[1])
    corner(0, peers[0])
    for load in loads:
        load.wait()
    lift_sides(0)
    take(3)
    forward(2, peers[2])
    corner(1, peers[1])
    lift_sides(1)
    finish(0, peers[0], 2)
    lift(across, peers[0], 2, closing=False)
    forward(3, peers[3])
    corner(2, peers[2])
    lift_sides(2)
    finish(3, peers[3], 1)
    lift(along_x, peers[3], 0, opening=False)
    lower(1)
    corner(3, peers[3])
    lift(along_y, peers[3], 1, opening=False)
    lower(2)
    for j in order:
        send_x(j)
    for j in order:
        send_y(j)
    for j in range(1, PIECES):
        finish(j, peers[j], 2)
        lift(across, peers[j], 2, opening=False, closing=j == 3)
    lower(0)
    for j in order:
        send_corner(j)
    for j in range(PIECES):
        finish(j, peers[j], 0)
    lift(cx)
    second(3)
    second(2)
    lower(3)
    third(3)
    second(1)
    second(0)
    third(2)
    third(1)
    total = third(0) + hidden_ref[...]
    copies.wait(("z_out", 1), z_in.at[1], (cx, peers[1]))
    copies.wait(("z_out", 2), z_in.at[3], (cx, peers[2]))
    total = total + z_in[1].astype(jnp.float32) + z_in[3].astype(jnp.float32)
    out_ref[...] = total.astype(jnp.bfloat16)
    copies.drain()


def experts_layer(partial_rows, layer_input, gain, router, ids, w_gate, w_up, w_down):
    rows, share = layer_input.shape
    width, units = w_gate.shape
    everyone = 2 * CHIPS * rows
    in_vmem = pl.BlockSpec(memory_space=pltpu.VMEM)
    anywhere = pl.BlockSpec(memory_space=pl.ANY)
    piece = pltpu.VMEM((PIECES, rows, share), jnp.bfloat16)
    half = pltpu.VMEM((PIECES, rows // 2, share), jnp.bfloat16)
    work = everyone * 6 * width * units
    return pl.pallas_call(
        layer_kernel,
        out_shape=jax.ShapeDtypeStruct((rows, share), jnp.bfloat16),
        in_specs=[in_vmem] * 5 + [anywhere] * 3,
        out_specs=in_vmem,
        scratch_shapes=[
            pltpu.VMEM((rows, share), jnp.float32),
            pltpu.VMEM((everyone, width), jnp.bfloat16),
            pltpu.VMEM((PIECES, 8, rows), jnp.float32),
            pltpu.VMEM((width, units), jnp.bfloat16),
            pltpu.VMEM((width, units), jnp.bfloat16),
            pltpu.VMEM((units, width), jnp.bfloat16),
            pltpu.VMEM((3, 2 * rows, units), jnp.float32),
            pltpu.VMEM((3, 2 * rows, units), jnp.float32),
            pltpu.VMEM((2 * rows, units), jnp.bfloat16),
            pltpu.VMEM((everyone, width), jnp.bfloat16),
            pltpu.VMEM((PIECES, CHIPS, rows, share), jnp.bfloat16),
        ]
        + [piece] * 5
        + [half] * 2
        + [piece] * 4
        + [pltpu.SemaphoreType.DMA((88,)), pltpu.SemaphoreType.DMA((88,))]
        + [pltpu.SemaphoreType.DMA((3,))],
        compiler_params=pltpu.CompilerParams(
            collective_id=2, has_side_effects=True, vmem_limit_bytes=VMEM_BYTES
        ),
        cost_estimate=pl.CostEstimate(
            flops=work, bytes_accessed=6 * width * units, transcendentals=0
        ),
        name="experts_layer",
    )(partial_rows, layer_input, gain, router, ids, w_gate, w_up, w_down)


def shards_dense(
    layer_input,
    queries,
    keys,
    values,
    gate_input,
    log_decay,
    prior_state,
    attn_gain,
    out_weight,
    moe_gain,
    router,
    expert_ids,
    w_gate,
    w_up,
    w_down,
):
    positions = queries.shape[0]
    heads_here = log_decay.shape[0]
    head_size = prior_state.shape[1]
    me = lax.axis_index("cx")
    query_vectors = queries.reshape(positions, heads_here, head_size)
    key_rows = keys.reshape(positions, heads_here, head_size)
    value_single_float = values.reshape(positions, heads_here, head_size).astype(jnp.float32)
    running_state = jnp.cumsum(log_decay, axis=1)
    trailing_rows = jnp.exp(running_state[:, -1:] - running_state)
    key_single_float = key_rows.astype(jnp.float32) * trailing_rows.T[:, :, None]
    within_block_state = jnp.einsum(
        "gpc,gpw->pcw", key_single_float, value_single_float, precision=highest_precision
    )
    total_decay = running_state[:, -1]
    coarse = lax.reduce_precision(total_decay, 8, 7)
    decay_row = jnp.concatenate(
        [coarse, total_decay - coarse, jnp.zeros((head_size - 2 * heads_here,), jnp.float32)]
    )
    extra = jnp.concatenate(
        [
            expert_ids.T.astype(jnp.float32),
            decay_row[None, :],
            jnp.zeros((13, head_size), jnp.float32),
        ]
    )
    state_rows = heads_here * head_size
    block = jnp.concatenate(
        [within_block_state.reshape(state_rows, head_size), extra]
    ).astype(jnp.bfloat16)
    gathered, all_ids = gather_states(block)
    decays = all_ids[:, 2, :]
    decays = decays[:, :heads_here] + decays[:, heads_here : 2 * heads_here]
    peers = decays.shape[0]
    spot = jnp.arange(peers)
    earlier = spot < me
    decays = jnp.where(earlier[:, None], decays, 0.0)
    later = spot[None, :] > spot[:, None]
    factor = jnp.exp(jnp.sum(jnp.where(later[:, :, None], decays[None], 0.0), axis=1))
    factor = jnp.where(earlier[:, None], factor, 0.0)
    all_states = gathered[:, :state_rows, :].reshape(peers, heads_here, head_size, head_size)
    incoming_state = jnp.exp(jnp.sum(decays, axis=0))[:, None, None] * prior_state + jnp.sum(
        factor[:, :, None, None] * all_states.astype(jnp.float32), axis=0
    )
    causal = (jnp.arange(positions)[:, None] >= jnp.arange(positions)[None, :])[None]
    spread = running_state[:, :, None] - running_state[:, None, :]
    weights = jnp.where(causal, jnp.exp(jnp.where(causal, spread, 0.0)), 0.0)
    scores = (
        jnp.einsum("thk,shk->hts", query_vectors, key_rows, preferred_element_type=jnp.float32)
        * weights
    )
    inner = jnp.einsum("hts,shv->thv", scores, value_single_float, precision=highest_precision)
    carried_contribution = jnp.exp(running_state).T[:, :, None] * jnp.einsum(
        "rxg,xgd->rxd",
        query_vectors.astype(jnp.float32),
        incoming_state,
        precision=highest_precision,
    )
    attended = inner + carried_contribution
    squares = jnp.mean(attended * attended, axis=-1, keepdims=True)
    gating = jax.nn.sigmoid(
        gate_input.astype(jnp.float32).reshape(positions, heads_here, head_size)
    )
    normed = (
        attended * lax.rsqrt(squares + epsilon) * attn_gain.reshape(heads_here, head_size) * gating
    )
    normed = normed.astype(jnp.bfloat16).reshape(positions, heads_here * head_size)
    partial_rows = jnp.dot(normed, out_weight, preferred_element_type=jnp.float32)
    return experts_layer(
        partial_rows, layer_input, moe_gain[None, :], router, all_ids, w_gate[0], w_up[0], w_down[0]
    )


def solution(mesh):
    placed = (
        P("cx", "tp"),
        P("cx", "tp"),
        P("cx", "tp"),
        P("cx", "tp"),
        P("cx", "tp"),
        P("tp", "cx"),
        P("tp", None, None),
        P("tp"),
        P("tp", None),
        P(),
        P(),
        P("cx", None),
        P("cx", None, "tp"),
        P("cx", None, "tp"),
        P("cx", "tp", None),
    )
    dense = mesh.shape["cx"] == 2 * CHIPS and mesh.shape["tp"] == PIECES
    shards = shards_dense if dense else shards_routed
    return jax.shard_map(
        shards, mesh=mesh, in_specs=placed, out_specs=P("cx", "tp"), check_vma=False
    )
```
